32 devices in a mesh: group: 2 (over x), row: 2 (over core), col: 8 (over z, y).
Axes of the slice: x: 2, y: 2, z: 4, core: 2. Of those that a mesh axis runs over, the one named last changes fastest.
Arguments:
- alignment: bfloat16 [256, 64, 256], P(('group', 'row'), 'col'), parts along dimension 0, may hold values from -6 to 6
- norm_mean: float32 [256, 64], P(('group', 'row'), 'col'), parts along dimension 0, may hold values from -3 to 3
- norm_inverse: float32 [256, 64], P(('group', 'row'), 'col'), parts along dimension 0, may hold values from 0.5 to 2
- norm_gain: float32 [256], replicated, may hold values from 0.5 to 1.5
- norm_shift: float32 [256], replicated, may hold values from -3 to 3
- input_weight: bfloat16 [256, 64], replicated, may hold values from -0.375 to 0.375
- input_bias: float32 [64], replicated, may hold values from -3 to 3
- output_weight: bfloat16 [1024, 128], replicated, may hold values from -0.1875 to 0.1875
- pair_cotangent: bfloat16 [64, 128, 128], P('col', 'group'), parts along dimension 1, may hold values from -6 to 6
- residue_mask: int32 [128], P('group'), parts along dimension 0, may hold values 0 or 1
- sequence_mask: int32 [256, 64], P(('group', 'row'), 'col'), parts along dimension 0, may hold values 0 or 1
Outputs:
- activation_grad: bfloat16 [256, 64, 256], P(('group', 'row'), 'col'), parts along dimension 0
- input_weight_grad: float32 [512, 64], P('group'), parts along dimension 0
- input_bias_grad: float32 [128], P('group'), parts along dimension 0
- output_weight_grad: float32 [2048, 128], P('group'), parts along dimension 0
- output_bias_grad: float32 [256], P('group'), parts along dimension 0
- gain_grad: float32 [512], P('group'), parts along dimension 0
- shift_grad: float32 [512], P('group'), parts along dimension 0
The draws below stay inside these ranges and needn't reach their ends.
There are 2 independent parts, one for each index of `group`. The reference program is written for one: setup_inputs(seed, part) draws one part's arguments, and reference() takes and returns one part's arrays. A program takes and returns all parts, laid end to end along the dimension named above; an argument that names none is the same for every part. Nothing has to cross between parts.
All inputs are finite; a program needn't handle non-finite values. No bound on the sum of `sequence_mask` on one device may be relied on, other than what follows from the above.
Results may differ from the reference program's by a relative error of at most 0.0075.
Values may be sent and summed in bfloat16 or wider, within the bound.
No kernel may reach another device: no remote copies, remote signals or barrier semaphores. Data moves between devices by JAX's collectives and lax.ppermute only.
A program may use at most 64 MiB of HBM per device.

```python
import math
import jax
import jax.numpy as jnp
from jax import lax

C = 256
P_SIZE = 32
Z = 128
RES_DEV = 8
SEQS = 128
RESIDUES = 64


def set_ends(result, key, low, largest):
    longest = result.shape.index(max(result.shape))
    spots = []
    for shift in (0, 1):
        where = [jax.random.randint(jax.random.fold_in(key, axis), (), 0, length) for axis, length in enumerate(result.shape)]
        where[longest] = (where[longest] + shift) % result.shape[longest]
        spots.append(tuple(where))
    return result.at[spots[0]].set(low).at[spots[1]].set(largest)


def shard_levels(key, extent, cuts, least, high):
    level = 1.0
    for axis_at, blocks in cuts:
        heights = jax.random.uniform(jax.random.fold_in(jax.random.fold_in(key, 6), axis_at), (blocks,), jnp.float32, least / len(cuts), high / len(cuts))
        level = level * jnp.repeat(jnp.exp(heights), extent[axis_at] // blocks).reshape((-1,) + (1,) * (len(extent) - 1 - axis_at))
    return level


def bell_draw(rng, shape, width, most, pieces=(), kind=jnp.bfloat16):
    loudness = shard_levels(rng, shape, pieces, -0.22, 0.18) if pieces else 1.0
    values = jax.random.normal(rng, shape, jnp.float32) * width * loudness
    return jnp.minimum(jnp.maximum(values, -most), most).astype(kind)


def setup_inputs(seed: int = 0, part: int = 0) -> dict:
    seeds = jax.random.split(jax.random.key(seed), 12)
    part_keys = jax.random.split(jax.random.fold_in(seeds[11], part), 12)
    return {
        "alignment": bell_draw(part_keys[0], (SEQS, RESIDUES, C), 1.0, 6.0, ((0, 2), (1, 8))),
        "norm_mean": bell_draw(part_keys[1], (SEQS, RESIDUES), 0.5, 3.0, ((0, 2), (1, 8)), jnp.float32),
        "norm_inverse": jnp.clip(jnp.exp(math.log(2.0) - 1.3862944 * jax.random.uniform(part_keys[2], (SEQS, RESIDUES), jnp.float32) ** shard_levels(part_keys[2], (SEQS, RESIDUES), ((0, 2), (1, 8)), -0.2, 0.2)), 0.5, 2.0),
        "norm_gain": jnp.clip(1.0 + 0.1 * jax.random.normal(seeds[3], (C,), jnp.float32), 0.5, 1.5),
        "norm_shift": bell_draw(seeds[4], (C,), 0.5, 3.0, (), jnp.float32),
        "input_weight": bell_draw(seeds[5], (C, 2 * P_SIZE), C ** -0.5, 0.375),
        "input_bias": bell_draw(seeds[6], (2 * P_SIZE,), 0.5, 3.0, (), jnp.float32),
        "output_weight": bell_draw(seeds[7], (P_SIZE * P_SIZE, Z), (P_SIZE * P_SIZE) ** -0.5, 0.1875),
        "pair_cotangent": bell_draw(part_keys[8], (RESIDUES, RESIDUES, Z), 1.0, 6.0, ((0, 8),)),
        "residue_mask": set_ends((jax.random.randint(part_keys[9], (RESIDUES,), 0, 8) < 7).astype(jnp.int32), jax.random.fold_in(part_keys[9], 1), 0, 1),
        "sequence_mask": set_ends((jax.random.randint(part_keys[10], (SEQS, RESIDUES), 0, 4) < 3).astype(jnp.int32), jax.random.fold_in(part_keys[10], 1), 0, 1),
    }


def normalize(alignment, norm_mean, norm_inverse, norm_gain, norm_shift):
    hatted = (alignment.astype(jnp.float32) - norm_mean[..., None]) * norm_inverse[..., None]
    normed = (hatted * norm_gain + norm_shift).astype(jnp.bfloat16)
    return hatted, normed


def project(normed, input_weight, input_bias, live):
    flat = normed.reshape(-1, normed.shape[-1])
    projected = jnp.dot(flat, input_weight, preferred_element_type=jnp.float32) + input_bias
    projected = projected.reshape(normed.shape[:-1] + (input_weight.shape[1],)) * live[..., None]
    return projected.astype(jnp.bfloat16)


def reference(alignment, norm_mean, norm_inverse, norm_gain, norm_shift, input_weight, input_bias, output_weight, pair_cotangent, residue_mask, sequence_mask):
    residue_float = residue_mask.astype(jnp.float32)
    live = sequence_mask.astype(jnp.float32) * residue_float[None, :]
    hatted, normed = normalize(alignment, norm_mean, norm_inverse, norm_gain, norm_shift)
    projected = project(normed, input_weight, input_bias, live)
    left = projected[..., :P_SIZE]
    right = projected[..., P_SIZE:]
    right_wide = right.astype(jnp.float32)

    def visit(carry, index):
        right_acc, weight_acc, bias_acc = carry
        offset = index * RES_DEV
        left_rows = lax.dynamic_slice_in_dim(left, offset, RES_DEV, 1).astype(jnp.float32)
        live_rows = lax.dynamic_slice_in_dim(live, offset, RES_DEV, 1)
        cot_rows = lax.dynamic_slice_in_dim(pair_cotangent, offset, RES_DEV, 0)
        mask_rows = lax.dynamic_slice_in_dim(residue_float, offset, RES_DEV, 0)
        counts = jnp.dot(live_rows.T, live, precision=lax.Precision.HIGHEST)
        scale = mask_rows[:, None] * residue_float[None, :] / jnp.maximum(counts, 1.0)
        pair_grad = cot_rows.astype(jnp.float32) * scale[..., None]
        pair_low = pair_grad.astype(jnp.bfloat16)
        outer_grad = jnp.dot(pair_low.reshape(-1, Z), output_weight.T, preferred_element_type=jnp.float32)
        outer_grad = outer_grad.astype(jnp.bfloat16).astype(jnp.float32).reshape(RES_DEV, RESIDUES, P_SIZE, P_SIZE)
        left_part = jnp.einsum('ijpq,sjq->sip', outer_grad, right_wide)
        right_acc = right_acc + jnp.einsum('ijpq,sip->sjq', outer_grad, left_rows)
        outer = jnp.einsum('sip,sjq->ijpq', left_rows, right_wide).reshape(-1, P_SIZE * P_SIZE)
        weight_acc = weight_acc + jnp.dot(outer.T, pair_low.reshape(-1, Z).astype(jnp.float32), precision=lax.Precision.HIGHEST)
        bias_acc = bias_acc + jnp.sum(pair_grad, axis=(0, 1))
        return (right_acc, weight_acc, bias_acc), left_part

    start_carry = (jnp.zeros((SEQS, RESIDUES, P_SIZE), jnp.float32), jnp.zeros((P_SIZE * P_SIZE, Z), jnp.float32), jnp.zeros((Z,), jnp.float32))
    indices = jnp.arange(RESIDUES // RES_DEV, dtype=jnp.int32)
    (right_grad, output_weight_grad, output_bias_grad), left_parts = lax.scan(visit, start_carry, indices)
    left_grad = jnp.transpose(left_parts, (1, 0, 2, 3)).reshape(SEQS, RESIDUES, P_SIZE)
    proj_grad = jnp.concatenate([left_grad, right_grad], axis=-1) * live[..., None]
    proj_low = proj_grad.astype(jnp.bfloat16).reshape(-1, 2 * P_SIZE)
    flat_normed = normed.reshape(-1, C)
    input_weight_grad = jnp.dot(flat_normed.T, proj_low, preferred_element_type=jnp.float32)
    input_bias_grad = jnp.sum(proj_grad, axis=(0, 1))
    normed_grad = jnp.dot(proj_low, input_weight.T, preferred_element_type=jnp.float32).reshape(SEQS, RESIDUES, C)
    gain_grad = jnp.sum(normed_grad * hatted, axis=(0, 1))
    shift_grad = jnp.sum(normed_grad, axis=(0, 1))
    hat_grad = normed_grad * norm_gain
    centered = hat_grad - jnp.mean(hat_grad, axis=-1, keepdims=True) - hatted * jnp.mean(hat_grad * hatted, axis=-1, keepdims=True)
    activation_grad = (norm_inverse[..., None] * centered).astype(jnp.bfloat16)
    return activation_grad, input_weight_grad, input_bias_grad, output_weight_grad, output_bias_grad, gain_grad, shift_grad
```

```python
import math

import jax
import jax.numpy as jnp
from jax import lax
from jax.experimental import pallas as pl
from jax.experimental.pallas import tpu as pltpu
from jax.sharding import PartitionSpec as P

C = 256
P_SIZE = 32
Z = 128


def normalize(alignment, norm_mean, norm_inverse, norm_gain, norm_shift):
    hatted = (alignment.astype(jnp.float32) - norm_mean[..., None]) * norm_inverse[..., None]
    normed = (hatted * norm_gain + norm_shift).astype(jnp.bfloat16)
    return (hatted, normed)


def project(normed, input_weight, input_bias, live):
    flat = normed.reshape(-1, normed.shape[-1])
    projected = jnp.dot(flat, input_weight, preferred_element_type=jnp.float32) + input_bias
    projected = projected.reshape(normed.shape[:-1] + (input_weight.shape[1],)) * live[..., None]
    return projected.astype(jnp.bfloat16)


def contract(left, right, counts, cotangent, pair_live, output_weight):
    sequence_count, row_count, _ = left.shape
    column_total = right.shape[1]
    width = math.gcd(column_total, 128)
    left_acc = jnp.zeros(left.shape, jnp.float32)
    weight_acc = jnp.zeros((P_SIZE * P_SIZE, Z), jnp.float32)
    bias_acc = jnp.zeros((Z,), jnp.float32)
    pieces = []
    for offset in range(0, column_total, width):
        right_cols = right[:, offset : offset + width]
        scale = pair_live[:, offset : offset + width] / jnp.maximum(
            counts[:, offset : offset + width], 1.0
        )
        pair_grad = cotangent[:, offset : offset + width].astype(jnp.float32) * scale[..., None]
        pair_low = pair_grad.astype(jnp.bfloat16).reshape(-1, Z)
        outer_grad = jnp.einsum(
            "ne,ke->nk", pair_low, output_weight, preferred_element_type=jnp.float32
        )
        outer_grad = outer_grad.astype(jnp.bfloat16).reshape(row_count, width, P_SIZE, P_SIZE)
        left_acc = left_acc + jnp.einsum(
            "ijpq,sjq->sip", outer_grad, right_cols, preferred_element_type=jnp.float32
        )
        pieces.append(
            jnp.einsum("ijpq,sip->sjq", outer_grad, left, preferred_element_type=jnp.float32)
        )
        outer = jnp.einsum(
            "sip,sjq->ijpq", left, right_cols, preferred_element_type=jnp.float32
        ).reshape(-1, P_SIZE * P_SIZE)
        outer_high = outer.astype(jnp.bfloat16)
        outer_rest = (outer - outer_high.astype(jnp.float32)).astype(jnp.bfloat16)
        weight_acc = weight_acc + jnp.einsum(
            "nk,ne->ke", outer_high, pair_low, preferred_element_type=jnp.float32
        )
        weight_acc = weight_acc + jnp.einsum(
            "nk,ne->ke", outer_rest, pair_low, preferred_element_type=jnp.float32
        )
        bias_acc = bias_acc + jnp.sum(pair_grad, axis=(0, 1))
    right_out = jnp.concatenate(pieces, axis=1)
    return (left_acc, right_out, weight_acc, bias_acc)


def general(
    alignment,
    norm_mean,
    norm_inverse,
    norm_gain,
    norm_shift,
    input_weight,
    input_bias,
    output_weight,
    pair_cotangent,
    residue_mask,
    sequence_mask,
):
    sequence_count, residue_count = sequence_mask.shape
    residue_total = residue_mask.shape[0]
    column = lax.axis_index("col")
    residue_float = residue_mask.astype(jnp.float32)
    own_residues = lax.dynamic_slice_in_dim(residue_float, column * residue_count, residue_count, 0)
    own_mask = lax.dynamic_slice_in_dim(residue_mask, column * residue_count, residue_count, 0)
    live_int = sequence_mask * own_mask[None, :]
    live = live_int.astype(jnp.float32)
    hatted, normed = normalize(alignment, norm_mean, norm_inverse, norm_gain, norm_shift)
    projected = project(normed, input_weight, input_bias, live)
    left = projected[..., :P_SIZE]
    right = projected[..., P_SIZE:]
    gathered, mask_cols = (
        lax.all_gather(
            right.reshape(sequence_count, residue_count * P_SIZE), "col", axis=1, tiled=True
        ),
        lax.all_gather(live_int, "col", axis=1, tiled=True),
    )
    right_all = gathered.reshape(sequence_count, residue_total, P_SIZE)
    partial_counts = jnp.dot(live.T, mask_cols.astype(jnp.float32), precision=lax.Precision.HIGHEST)
    counts = lax.psum(partial_counts, "row")
    pair_live = own_residues[:, None] * residue_float[None, :]
    left_grad, right_part, weight_out, bias_out = contract(
        left, right_all, counts, pair_cotangent, pair_live, output_weight
    )
    bias_out = bias_out / lax.axis_size("row")
    summed = lax.psum_scatter(
        right_part.reshape(sequence_count, residue_total * P_SIZE),
        "col",
        scatter_dimension=1,
        tiled=True,
    )
    right_grad = summed.reshape(sequence_count, residue_count, P_SIZE)
    proj_grad = jnp.concatenate([left_grad, right_grad], axis=-1) * live[..., None]
    proj_low = proj_grad.astype(jnp.bfloat16).reshape(-1, 2 * P_SIZE)
    flat_normed = normed.reshape(-1, C)
    weight_part = jnp.einsum("nc,nk->ck", flat_normed, proj_low, preferred_element_type=jnp.float32)
    bias_part = jnp.sum(proj_grad, axis=(0, 1))
    normed_grad = jnp.einsum(
        "nk,ck->nc", proj_low, input_weight, preferred_element_type=jnp.float32
    ).reshape(hatted.shape)
    gain_part = jnp.sum(normed_grad * hatted, axis=(0, 1))
    shift_part = jnp.sum(normed_grad, axis=(0, 1))
    hat_grad = normed_grad * norm_gain
    centered = (
        hat_grad
        - jnp.mean(hat_grad, axis=-1, keepdims=True)
        - hatted * jnp.mean(hat_grad * hatted, axis=-1, keepdims=True)
    )
    activation_grad = (norm_inverse[..., None] * centered).astype(jnp.bfloat16)
    totals = lax.psum(
        (weight_part, bias_part, gain_part, shift_part, weight_out, bias_out), ("row", "col")
    )
    return (activation_grad, totals[0], totals[1], totals[4], totals[5], totals[2], totals[3])


LANES = 128
PROJ_ROWS = 256
MASK_AT = 256
TURNED_AT = 272
SLICE_AT = 336
MESSAGE = 400
SMALL_AT = 256
PARTIAL = 288
VMEM = pltpu.CompilerParams(vmem_limit_bytes=48 * 1024 * 1024)
F32 = jnp.float32
BF16 = jnp.bfloat16


def dot_nt(a, b):
    return lax.dot_general(a, b, (((1,), (1,)), ((), ())), preferred_element_type=F32)


def dot_nn(a, b):
    return lax.dot_general(a, b, (((1,), (0,)), ((), ())), preferred_element_type=F32)


def low_lanes(shape):
    return lax.broadcasted_iota(jnp.int32, shape, 1) < LANES // 2


def swap_halves(x):
    return pltpu.roll(x, LANES // 2, 1)


def columns_of(square, rows):
    at = 0
    for block in rows:
        square[at : at + block.shape[0], : block.shape[1]] = block
        at += block.shape[0]
    return square[...].T


def spread(wide, alignment):
    values = alignment[...].astype(F32)
    for h in range(2):
        wide[h, 0 : values.shape[0] * values.shape[1], :] = values[
            :, :, h * LANES : (h + 1) * LANES
        ].reshape(-1, LANES)


def strided(wide, start, size, stride):
    return jnp.concatenate([wide[h, pl.ds(start, size, stride=stride), :] for h in range(2)], axis=1)


def prepare(
    column, residue, alignment, mean, inverse, gain, shift, weight, bias, mask, mate, cotangent, *rest
):
    count = (len(rest) - 4) // 1
    messages, (wide, packed, cot, turned) = rest[:count], rest[count:]
    col = column[0]
    seqs, own, channels = alignment.shape
    square = cot.at[0:LANES, :]
    stats = columns_of(
        square, [mean[...], inverse[...], jnp.broadcast_to(bias[...], (8, bias.shape[1]))]
    )
    row = lax.broadcasted_iota(jnp.int32, (own, LANES), 0)
    present = jnp.zeros((own, LANES), F32)
    for r in range(own):
        present = jnp.where(row == r, residue[col * own + r].astype(F32), present)
    live = jnp.concatenate([mask[...], mate[...]], axis=1).astype(F32) * present
    spread(wide, alignment)
    for r in range(own):
        hatted = (strided(wide, r, seqs, own) - stats[:seqs, r : r + 1]) * stats[
            :seqs, own + r : own + r + 1
        ]
        normed = (hatted * gain[...] + shift[...]).astype(BF16)
        projected = dot_nt(weight[...], normed) + stats[: 2 * P_SIZE, 2 * own : 2 * own + 1]
        projected = projected * live[r : r + 1, :seqs]
        packed[pl.ds(r, P_SIZE, stride=own), :] = jnp.concatenate(
            [projected[:P_SIZE], projected[P_SIZE:]], axis=1
        )
    shared = packed[...].astype(BF16)
    masks = jnp.concatenate([live, present], axis=0).astype(BF16)
    total = cotangent.shape[1]
    cot[...] = cotangent[...].astype(F32).reshape(own * total, Z)
    for i in range(own // 2):
        pair = jnp.concatenate(
            [cot[i * total : (i + 1) * total, :], cot[(i + own // 2) * total : (i + own // 2 + 1) * total, :]],
            axis=0,
        )
        turned[i] = pair.T.astype(BF16)
    depth = Z // count
    for k in range(count):
        peer = col ^ k
        out = messages[k]
        out[0:PROJ_ROWS, :] = shared
        out[MASK_AT:TURNED_AT, :] = masks
        out[TURNED_AT:SLICE_AT, :] = jnp.concatenate(
            [cot[pl.ds(own * peer + j, own, stride=total), :] for j in range(own)], axis=0
        ).astype(BF16)
        for i in range(own // 2):
            out[SLICE_AT + i * depth : SLICE_AT + (i + 1) * depth, :] = turned[
                i, pl.ds(pl.multiple_of(peer * depth, depth), depth), :
            ]


def interleave(product, target, group, at):
    half = LANES // 2
    low = low_lanes((P_SIZE, LANES))
    for a in range(0, product.shape[0] // P_SIZE, 2):
        for b in range(0, group, 2):
            first = product[a * P_SIZE : (a + 1) * P_SIZE, b * half : (b + 2) * half]
            second = product[(a + 1) * P_SIZE : (a + 2) * P_SIZE, b * half : (b + 2) * half]
            lanes = slice((at + a) * half, (at + a + 2) * half)
            target[b * P_SIZE : (b + 1) * P_SIZE, lanes] = jnp.where(
                low, first, swap_halves(second)
            ).astype(BF16)
            target[(b + 1) * P_SIZE : (b + 2) * P_SIZE, lanes] = jnp.where(
                low, swap_halves(first), second
            ).astype(BF16)


def work(
    column, cotangent, out_weight, alignment, mean, inverse, gain, shift, weight, *rest
):
    count = len(rest) - 15
    messages = rest[:count]
    activation, partial = rest[count : count + 2]
    (every, live_all, present_all, turned, slices, grad_own, grad_turned, grad_slice, left_outer, right_outer, right_rows, mixed, wide) = rest[count + 2 :]
    col = column[0]
    seqs, own, channels = alignment.shape
    total = cotangent.shape[1]
    depth = Z // count
    half = LANES // 2
    pairs = own // 2
    for k in range(count):
        peer = col ^ k
        at = pl.multiple_of(peer * own, own)
        message = messages[k]
        block = message[0:PROJ_ROWS, :].astype(F32)
        for q in range(P_SIZE):
            every[pl.ds(q * total + at, own), :] = block[q * own : (q + 1) * own]
        masks = message[MASK_AT:TURNED_AT, :].astype(F32)
        live_all[pl.ds(at, own), :] = masks[:own]
        present_all[pl.ds(at, own), :] = masks[own:]
        block = message[TURNED_AT:SLICE_AT, :].astype(F32)
        for j in range(own):
            turned[pl.ds(j * total + at, own), :] = block[j * own : (j + 1) * own]
        slices[peer] = message[SLICE_AT:MESSAGE, :]
    live = live_all[...].astype(BF16)
    present = present_all[...].astype(BF16)
    masks = messages[0][MASK_AT:TURNED_AT, :]
    live_own = masks[:own].astype(F32)
    present_own = masks[own:]

    def scale_of(live_other, present_other):
        counts = dot_nt(live, live_other)
        return dot_nt(present, present_other) * (1.0 / LANES) / jnp.maximum(counts, 1.0)

    scale_own = scale_of(masks[:own], present_own)
    scale_twice = scale_of(
        jnp.concatenate([live, live], axis=0), jnp.concatenate([present, present], axis=0)
    )
    for i in range(own):
        rows = slice(i * total, (i + 1) * total)
        grad_own[rows, :] = (cotangent[i].astype(F32) * scale_own[:, i : i + 1]).astype(BF16)
        grad_turned[rows, :] = (turned[rows, :] * scale_own[:, i : i + 1]).astype(BF16)
    low = low_lanes((own, LANES))
    bias_acc = jnp.zeros((depth, LANES), F32)
    for c in range(count):
        tile = scale_twice[c * own : (c + 1) * own]
        tile = jnp.where(low, tile, jnp.concatenate([tile[pairs:], tile[:pairs]], axis=0))
        for i in range(pairs):
            piece = slices[c, i * depth : (i + 1) * depth, :].astype(F32) * tile[i : i + 1, :]
            bias_acc = bias_acc + piece
            grad_slice[(c * pairs + i) * depth : (c * pairs + i + 1) * depth, :] = piece.astype(BF16)

    wide[0] = out_weight[...].astype(F32)
    eight = 8
    for a in range(0, P_SIZE, eight):
        rows = slice(a * P_SIZE, (a + eight) * P_SIZE)
        by_second = jnp.concatenate(
            [wide[0, pl.ds(q, P_SIZE, stride=P_SIZE), :] for q in range(a, a + eight)], axis=0
        ).astype(BF16)
        interleave(dot_nt(by_second, grad_own[...]), left_outer, own, a)
        interleave(dot_nt(out_weight[rows, :], grad_turned[...]), right_outer, own, a)
    gathered = every[...].astype(BF16)
    left_grad = swap_halves(dot_nn(left_outer[...], gathered))
    right_grad = dot_nn(right_outer[...], gathered)

    square = wide.at[0, 0:LANES, :]
    stats = columns_of(square, [mean[...], inverse[...]])
    spread(wide, alignment)
    input_acc = jnp.zeros((2 * P_SIZE, channels), F32)
    proj_acc = jnp.zeros((2 * P_SIZE, seqs), F32)
    gain_acc = jnp.zeros((1, channels), F32)
    shift_acc = jnp.zeros((1, channels), F32)
    for r in range(own):
        spot = pl.ds(r, seqs, stride=own)
        scale = stats[:seqs, own + r : own + r + 1]
        hatted = (strided(wide, r, seqs, own) - stats[:seqs, r : r + 1]) * scale
        normed = (hatted * gain[...] + shift[...]).astype(BF16)
        rows = slice(r * P_SIZE, (r + 1) * P_SIZE)
        proj_grad = jnp.concatenate([left_grad[rows, :seqs], right_grad[rows, :seqs]], axis=0)
        proj_grad = proj_grad * live_own[r : r + 1, :seqs]
        proj_acc = proj_acc + proj_grad
        input_acc = input_acc + dot_nn(proj_grad.astype(BF16), normed)
        normed_grad = dot_nn(proj_grad.T.astype(BF16), weight[...])
        gain_acc = gain_acc + jnp.sum(normed_grad * hatted, axis=0, keepdims=True)
        shift_acc = shift_acc + jnp.sum(normed_grad, axis=0, keepdims=True)
        hat_grad = normed_grad * gain[...]
        first = jnp.sum(hat_grad, axis=1, keepdims=True) * (1.0 / channels)
        second = jnp.sum(hat_grad * hatted, axis=1, keepdims=True) * (1.0 / channels)
        result = scale * (hat_grad - first - hatted * second)
        for h in range(2):
            wide[h, spot, :] = result[:, h * LANES : (h + 1) * LANES]
    activation[...] = jnp.concatenate(
        [wide[h, 0 : seqs * own, :].reshape(seqs, own, LANES) for h in range(2)], axis=2
    ).astype(BF16)

    right_rows[0:total, :] = jnp.zeros((total, P_SIZE * half), BF16)
    right_rows[2 * total : 3 * total, :] = jnp.zeros((total, P_SIZE * half), BF16)
    low = low_lanes((total, LANES))
    for q in range(0, P_SIZE, 2):
        first = every[q * total : (q + 1) * total, :]
        second = every[(q + 1) * total : (q + 2) * total, :]
        right_rows[total : 2 * total, q * half : (q + 2) * half] = jnp.where(
            low, swap_halves(first), second
        ).astype(BF16)
    low = low_lanes((P_SIZE, LANES))
    none = jnp.zeros((P_SIZE, LANES), BF16)
    weight_acc = jnp.zeros((LANES, LANES), F32)
    quarter = 4
    for top in range(2):
        right_side = right_rows[(1 - top) * total : (3 - top) * total, :]
        for c0 in range(0, count, quarter):
            span = quarter * pairs * depth
            mixed[...] = dot_nn(
                grad_slice[c0 * pairs * depth : c0 * pairs * depth + span, :], right_side
            ).astype(BF16)
            for c in range(quarter):
                for i in range(pairs):
                    at = (c * pairs + i) * depth
                    lhs = jnp.concatenate(
                        [mixed[at : at + depth, a * 256 : (a + 1) * 256] for a in range(8)], axis=0
                    )
                    left = every[pl.ds((c0 + c) * own + top * pairs + i, P_SIZE, stride=total), :]
                    left = jnp.where(low, left, 0.0)
                    moved = swap_halves(left).astype(BF16)
                    left = left.astype(BF16)
                    rhs = jnp.concatenate(
                        [
                            jnp.concatenate([left, none], axis=1),
                            jnp.concatenate([moved, none], axis=1),
                            jnp.concatenate([none, left], axis=1),
                            jnp.concatenate([none, moved], axis=1),
                        ],
                        axis=0,
                    )
                    weight_acc = weight_acc + dot_nt(lhs, rhs)

    square[...] = jnp.zeros((LANES, LANES), F32)
    square[0 : 2 * P_SIZE, :seqs] = proj_acc
    square[half : half + depth, :] = bias_acc
    sums = jnp.sum(square[...].T, axis=0, keepdims=True)
    small = jnp.concatenate(
        [gain_acc[:, :LANES], gain_acc[:, LANES:], shift_acc[:, :LANES], shift_acc[:, LANES:], sums, jnp.zeros((11, LANES), F32)],
        axis=0,
    )
    high = small.astype(BF16)
    rest_of = (small - high.astype(F32)).astype(BF16)
    whole = jnp.concatenate(
        [weight_acc.astype(BF16), input_acc[:, :LANES].astype(BF16), input_acc[:, LANES:].astype(BF16), high, rest_of],
        axis=0,
    )
    for k in range(count):
        partial[k] = whole


def finish(own, mate, input_out, bias_out, weight_out, out_bias_out, gain_out, shift_out):
    count = own.shape[0]
    depth = Z // count
    input_acc = jnp.zeros((LANES, LANES), F32)
    small_acc = jnp.zeros((16, LANES), F32)
    lane = lax.broadcasted_iota(jnp.int32, (1, LANES), 1)
    out_bias = jnp.zeros((1, LANES), F32)
    pieces = []
    for k in range(count):
        mine = own[k].astype(F32)
        both = mine + mate[k].astype(F32)
        pieces.append(both[:LANES])
        input_acc = input_acc + both[LANES:SMALL_AT]
        small_acc = small_acc + (both[SMALL_AT : SMALL_AT + 16] + both[SMALL_AT + 16 :])
        bias = mine[SMALL_AT + 4 : SMALL_AT + 5] + mine[SMALL_AT + 20 : SMALL_AT + 21]
        bias = pltpu.roll(bias, (k * depth + LANES // 2) % LANES, 1)
        out_bias = jnp.where((lane >= k * depth) & (lane < (k + 1) * depth), bias, out_bias)
    for a in range(8):
        turned = jnp.concatenate([p[a * depth : (a + 1) * depth] for p in pieces], axis=0).T
        for b in range(4):
            weight_out[pl.ds(4 * a + b, P_SIZE, stride=P_SIZE), :] = turned[b * P_SIZE : (b + 1) * P_SIZE]
    input_out[:, :LANES] = input_acc[: LANES // 2]
    input_out[:, LANES:] = input_acc[LANES // 2 :]
    gain_out[:, :LANES] = small_acc[0:1]
    gain_out[:, LANES:] = small_acc[1:2]
    shift_out[:, :LANES] = small_acc[2:3]
    shift_out[:, LANES:] = small_acc[3:4]
    bias_out[...] = small_acc[4:5, : LANES // 2]
    out_bias_out[...] = out_bias


def shape(dims, dtype):
    return jax.ShapeDtypeStruct(dims, dtype)


def tiled(
    alignment,
    norm_mean,
    norm_inverse,
    norm_gain,
    norm_shift,
    input_weight,
    input_bias,
    output_weight,
    pair_cotangent,
    residue_mask,
    sequence_mask,
):
    count = lax.axis_size("col")
    seqs, own, channels = alignment.shape
    total = pair_cotangent.shape[1]
    column = lax.axis_index("col").reshape(1).astype(jnp.int32)
    mask = sequence_mask.T
    mate = lax.ppermute(mask, "row", [(0, 1), (1, 0)])
    mean, inverse = norm_mean.T, norm_inverse.T
    gain, shift = norm_gain[None, :], norm_shift[None, :]
    weight = input_weight.T
    smem = pl.BlockSpec(memory_space=pltpu.SMEM)
    vmem = pl.BlockSpec(memory_space=pltpu.VMEM)
    messages = pl.pallas_call(
        prepare,
        out_shape=[shape((MESSAGE, LANES), BF16)] * count,
        in_specs=[smem, smem] + [vmem] * 10,
        out_specs=[vmem] * count,
        scratch_shapes=[
            pltpu.VMEM((2, seqs * own, LANES), F32),
            pltpu.VMEM((PROJ_ROWS, LANES), F32),
            pltpu.VMEM((own * total, Z), F32),
            pltpu.VMEM((own // 2, Z, LANES), BF16),
        ],
        compiler_params=VMEM,
        name="prepare",
    )(column, residue_mask, alignment, mean, inverse, gain, shift, weight, input_bias[None, :], mask, mate, pair_cotangent)
    received = [messages[0]] + [
        lax.ppermute(messages[k], "col", [(c, c ^ k) for c in range(count)]) for k in range(1, count)
    ]
    activation, partial = pl.pallas_call(
        work,
        out_shape=[shape(alignment.shape, BF16), shape((count, PARTIAL, LANES), BF16)],
        in_specs=[smem] + [vmem] * (8 + count),
        out_specs=[vmem] * 2,
        scratch_shapes=[
            pltpu.VMEM((P_SIZE * total, LANES), F32),
            pltpu.VMEM((total, LANES), F32),
            pltpu.VMEM((total, LANES), F32),
            pltpu.VMEM((own * total, Z), F32),
            pltpu.VMEM((count, MESSAGE - SLICE_AT, LANES), BF16),
            pltpu.VMEM((own * total, Z), BF16),
            pltpu.VMEM((own * total, Z), BF16),
            pltpu.VMEM((count * (MESSAGE - SLICE_AT), LANES), BF16),
            pltpu.VMEM((own * P_SIZE, P_SIZE * total), BF16),
            pltpu.VMEM((own * P_SIZE, P_SIZE * total), BF16),
            pltpu.VMEM((3 * total, P_SIZE * seqs), BF16),
            pltpu.VMEM((4 * (MESSAGE - SLICE_AT), P_SIZE * seqs), BF16),
            pltpu.VMEM((2, P_SIZE * P_SIZE, LANES), F32),
        ],
        compiler_params=VMEM,
        name="work",
    )(column, pair_cotangent, output_weight, alignment, mean, inverse, gain, shift, weight, *received)
    ours = lax.all_to_all(partial, "col", 0, 0)
    theirs = lax.ppermute(ours, "row", [(0, 1), (1, 0)])
    input_grad, bias_grad, weight_grad, out_bias_grad, gain_grad, shift_grad = pl.pallas_call(
        finish,
        out_shape=[
            shape((2 * P_SIZE, channels), F32),
            shape((1, 2 * P_SIZE), F32),
            shape((P_SIZE * P_SIZE, Z), F32),
            shape((1, Z), F32),
            shape((1, channels), F32),
            shape((1, channels), F32),
        ],
        in_specs=[vmem] * 2,
        out_specs=[vmem] * 6,
        compiler_params=VMEM,
        name="finish",
    )(ours, theirs)
    return (activation, input_grad.T, bias_grad[0], weight_grad, out_bias_grad[0], gain_grad[0], shift_grad[0])


def local(*args):
    alignment, cotangent = args[0], args[8]
    seqs, own, channels = alignment.shape
    total = cotangent.shape[1]
    count = lax.axis_size("col")
    fits = (
        2 * seqs == LANES
        and 2 * total == LANES
        and own == 8
        and channels == 2 * LANES
        and count == 8
        and lax.axis_size("row") == 2
    )
    return tiled(*args) if fits else general(*args)


def solution(mesh):
    in_specs = (
        P(("group", "row"), "col", None),
        P(("group", "row"), "col"),
        P(("group", "row"), "col"),
        P(),
        P(),
        P(),
        P(),
        P(),
        P("col", "group", None),
        P("group"),
        P(("group", "row"), "col"),
    )
    out_specs = (
        P(("group", "row"), "col", None),
        P("group", None),
        P("group"),
        P("group", None),
        P("group"),
        P("group"),
        P("group"),
    )
    return jax.shard_map(local, mesh=mesh, in_specs=in_specs, out_specs=out_specs, check_vma=False)
```

```python
import math

import jax
import jax.numpy as jnp
from jax import lax
from jax.experimental import pallas as pl
from jax.experimental.pallas import tpu as pltpu
from jax.sharding import PartitionSpec as P

C = 256
P_SIZE = 32
Z = 128


def normalize(alignment, norm_mean, norm_inverse, norm_gain, norm_shift):
    hatted = (alignment.astype(jnp.float32) - norm_mean[..., None]) * norm_inverse[..., None]
    normed = (hatted * norm_gain + norm_shift).astype(jnp.bfloat16)
    return (hatted, normed)


def project(normed, input_weight, input_bias, live):
    flat = normed.reshape(-1, normed.shape[-1])
    projected = jnp.dot(flat, input_weight, preferred_element_type=jnp.float32) + input_bias
    projected = projected.reshape(normed.shape[:-1] + (input_weight.shape[1],)) * live[..., None]
    return projected.astype(jnp.bfloat16)


def contract(left, right, counts, cotangent, pair_live, output_weight):
    sequence_count, row_count, _ = left.shape
    column_total = right.shape[1]
    width = math.gcd(column_total, 128)
    left_acc = jnp.zeros(left.shape, jnp.float32)
    weight_acc = jnp.zeros((P_SIZE * P_SIZE, Z), jnp.float32)
    bias_acc = jnp.zeros((Z,), jnp.float32)
    pieces = []
    for offset in range(0, column_total, width):
        right_cols = right[:, offset : offset + width]
        scale = pair_live[:, offset : offset + width] / jnp.maximum(
            counts[:, offset : offset + width], 1.0
        )
        pair_grad = cotangent[:, offset : offset + width].astype(jnp.float32) * scale[..., None]
        pair_low = pair_grad.astype(jnp.bfloat16).reshape(-1, Z)
        outer_grad = jnp.einsum(
            "ne,ke->nk", pair_low, output_weight, preferred_element_type=jnp.float32
        )
        outer_grad = outer_grad.astype(jnp.bfloat16).reshape(row_count, width, P_SIZE, P_SIZE)
        left_acc = left_acc + jnp.einsum(
            "ijpq,sjq->sip", outer_grad, right_cols, preferred_element_type=jnp.float32
        )
        pieces.append(
            jnp.einsum("ijpq,sip->sjq", outer_grad, left, preferred_element_type=jnp.float32)
        )
        outer = jnp.einsum(
            "sip,sjq->ijpq", left, right_cols, preferred_element_type=jnp.float32
        ).reshape(-1, P_SIZE * P_SIZE)
        outer_high = outer.astype(jnp.bfloat16)
        outer_rest = (outer - outer_high.astype(jnp.float32)).astype(jnp.bfloat16)
        weight_acc = weight_acc + jnp.einsum(
            "nk,ne->ke", outer_high, pair_low, preferred_element_type=jnp.float32
        )
        weight_acc = weight_acc + jnp.einsum(
            "nk,ne->ke", outer_rest, pair_low, preferred_element_type=jnp.float32
        )
        bias_acc = bias_acc + jnp.sum(pair_grad, axis=(0, 1))
    right_out = jnp.concatenate(pieces, axis=1)
    return (left_acc, right_out, weight_acc, bias_acc)


def general(
    alignment,
    norm_mean,
    norm_inverse,
    norm_gain,
    norm_shift,
    input_weight,
    input_bias,
    output_weight,
    pair_cotangent,
    residue_mask,
    sequence_mask,
):
    sequence_count, residue_count = sequence_mask.shape
    residue_total = residue_mask.shape[0]
    column = lax.axis_index("col")
    residue_float = residue_mask.astype(jnp.float32)
    own_residues = lax.dynamic_slice_in_dim(residue_float, column * residue_count, residue_count, 0)
    own_mask = lax.dynamic_slice_in_dim(residue_mask, column * residue_count, residue_count, 0)
    live_int = sequence_mask * own_mask[None, :]
    live = live_int.astype(jnp.float32)
    hatted, normed = normalize(alignment, norm_mean, norm_inverse, norm_gain, norm_shift)
    projected = project(normed, input_weight, input_bias, live)
    left = projected[..., :P_SIZE]
    right = projected[..., P_SIZE:]
    gathered, mask_cols = (
        lax.all_gather(
            right.reshape(sequence_count, residue_count * P_SIZE), "col", axis=1, tiled=True
        ),
        lax.all_gather(live_int, "col", axis=1, tiled=True),
    )
    right_all = gathered.reshape(sequence_count, residue_total, P_SIZE)
    partial_counts = jnp.dot(live.T, mask_cols.astype(jnp.float32), precision=lax.Precision.HIGHEST)
    counts = lax.psum(partial_counts, "row")
    pair_live = own_residues[:, None] * residue_float[None, :]
    left_grad, right_part, weight_out, bias_out = contract(
        left, right_all, counts, pair_cotangent, pair_live, output_weight
    )
    bias_out = bias_out / lax.axis_size("row")
    summed = lax.psum_scatter(
        right_part.reshape(sequence_count, residue_total * P_SIZE),
        "col",
        scatter_dimension=1,
        tiled=True,
    )
    right_grad = summed.reshape(sequence_count, residue_count, P_SIZE)
    proj_grad = jnp.concatenate([left_grad, right_grad], axis=-1) * live[..., None]
    proj_low = proj_grad.astype(jnp.bfloat16).reshape(-1, 2 * P_SIZE)
    flat_normed = normed.reshape(-1, C)
    weight_part = jnp.einsum("nc,nk->ck", flat_normed, proj_low, preferred_element_type=jnp.float32)
    bias_part = jnp.sum(proj_grad, axis=(0, 1))
    normed_grad = jnp.einsum(
        "nk,ck->nc", proj_low, input_weight, preferred_element_type=jnp.float32
    ).reshape(hatted.shape)
    gain_part = jnp.sum(normed_grad * hatted, axis=(0, 1))
    shift_part = jnp.sum(normed_grad, axis=(0, 1))
    hat_grad = normed_grad * norm_gain
    centered = (
        hat_grad
        - jnp.mean(hat_grad, axis=-1, keepdims=True)
        - hatted * jnp.mean(hat_grad * hatted, axis=-1, keepdims=True)
    )
    activation_grad = (norm_inverse[..., None] * centered).astype(jnp.bfloat16)
    totals = lax.psum(
        (weight_part, bias_part, gain_part, shift_part, weight_out, bias_out), ("row", "col")
    )
    return (activation_grad, totals[0], totals[1], totals[4], totals[5], totals[2], totals[3])


LANES = 128
PROJ_ROWS = 256
MASK_AT = 256
TURNED_AT = 272
SLICE_AT = 336
MESSAGE = 400
PARTIAL = 136
SENT = 144
VMEM = pltpu.CompilerParams(vmem_limit_bytes=48 * 1024 * 1024)
F32 = jnp.float32
BF16 = jnp.bfloat16


def dot_nt(a, b):
    return lax.dot_general(a, b, (((1,), (1,)), ((), ())), preferred_element_type=F32)


def dot_nn(a, b):
    return lax.dot_general(a, b, (((1,), (0,)), ((), ())), preferred_element_type=F32)


def low_lanes(shape):
    return lax.broadcasted_iota(jnp.int32, shape, 1) < LANES // 2


def swap_halves(x):
    return pltpu.roll(x, LANES // 2, 1)


def columns_of(square, rows):
    at = 0
    for block in rows:
        square[at : at + block.shape[0], : block.shape[1]] = block
        at += block.shape[0]
    return square[...].T


def spread(wide, alignment):
    values = alignment[...].astype(F32)
    for h in range(2):
        wide[h, 0 : values.shape[0] * values.shape[1], :] = values[
            :, :, h * LANES : (h + 1) * LANES
        ].reshape(-1, LANES)


def strided(wide, start, size, stride):
    return jnp.concatenate([wide[h, pl.ds(start, size, stride=stride), :] for h in range(2)], axis=1)


def fetch(sources, targets, arrived):
    copies = [pltpu.make_async_copy(s, t, arrived.at[i]) for i, (s, t) in enumerate(zip(sources, targets))]
    for copy in copies:
        copy.start()
    return copies


def prepare(column, residue, mate, *rest):
    count = len(rest) - 23
    sources, messages, targets = rest[:9], rest[9 : 9 + count], rest[9 + count : 18 + count]
    wide, packed, cot, turned, arrived = rest[18 + count :]
    alignment, mean, inverse, gain, shift, weight, bias, mask, cotangent = targets
    for copy in fetch(sources, targets, arrived):
        copy.wait()
    col = column[0]
    seqs, own, channels = alignment.shape
    square = cot.at[0:LANES, :]
    stats = columns_of(
        square, [mean[...], inverse[...], jnp.broadcast_to(bias[...], (8, bias.shape[1]))]
    )
    row = lax.broadcasted_iota(jnp.int32, (own, LANES), 0)
    present = jnp.zeros((own, LANES), F32)
    for r in range(own):
        present = jnp.where(row == r, residue[col * own + r].astype(F32), present)
    live = jnp.concatenate([mask[...], mate[...]], axis=1).astype(F32) * present
    spread(wide, alignment)
    for r in range(own):
        hatted = (strided(wide, r, seqs, own) - stats[:seqs, r : r + 1]) * stats[
            :seqs, own + r : own + r + 1
        ]
        normed = (hatted * gain[...] + shift[...]).astype(BF16)
        projected = dot_nt(weight[...], normed) + stats[: 2 * P_SIZE, 2 * own : 2 * own + 1]
        projected = projected * live[r : r + 1, :seqs]
        packed[pl.ds(r, P_SIZE, stride=own), :] = jnp.concatenate(
            [projected[:P_SIZE], projected[P_SIZE:]], axis=1
        )
    shared = packed[...].astype(BF16)
    masks = jnp.concatenate([live, present], axis=0).astype(BF16)
    total = cotangent.shape[1]
    cot[...] = cotangent[...].astype(F32).reshape(own * total, Z)
    for i in range(own // 2):
        pair = jnp.concatenate(
            [cot[i * total : (i + 1) * total, :], cot[(i + own // 2) * total : (i + own // 2 + 1) * total, :]],
            axis=0,
        )
        turned[i] = pair.T.astype(BF16)
    depth = Z // count
    for k in range(count):
        peer = col ^ k
        out = messages[k]
        out[0:PROJ_ROWS, :] = shared
        out[MASK_AT:TURNED_AT, :] = masks
        out[TURNED_AT:SLICE_AT, :] = jnp.concatenate(
            [cot[pl.ds(own * peer + j, own, stride=total), :] for j in range(own)], axis=0
        ).astype(BF16)
        for i in range(own // 2):
            out[SLICE_AT + i * depth : SLICE_AT + (i + 1) * depth, :] = turned[
                i, pl.ds(pl.multiple_of(peer * depth, depth), depth), :
            ]


def interleave(product, target, group, at):
    half = LANES // 2
    low = low_lanes((P_SIZE, LANES))
    for a in range(0, product.shape[0] // P_SIZE, 2):
        for b in range(0, group, 2):
            first = product[a * P_SIZE : (a + 1) * P_SIZE, b * half : (b + 2) * half]
            second = product[(a + 1) * P_SIZE : (a + 2) * P_SIZE, b * half : (b + 2) * half]
            lanes = slice((at + a) * half, (at + a + 2) * half)
            target[b * P_SIZE : (b + 1) * P_SIZE, lanes] = jnp.where(
                low, first, swap_halves(second)
            ).astype(BF16)
            target[(b + 1) * P_SIZE : (b + 2) * P_SIZE, lanes] = jnp.where(
                low, swap_halves(first), second
            ).astype(BF16)


def quad_members(quad):
    base = quad // 2 * 8 + quad % 2 * 2
    return ((base, base + 4), (base + 1, base + 5))


def work(place, *rest):
    count = len(rest) - 33
    messages, sources = rest[:count], rest[count : count + 8]
    activation, keep, give = rest[count + 8 : count + 11]
    targets = rest[count + 11 : count + 19]
    (every, live_all, present_all, turned, slices, grad_own, grad_turned, grad_slice, left_outer, right_outer, corner, mixed, wide, arrived) = rest[count + 19 :]
    cotangent, out_weight, alignment, mean, inverse, gain, shift, weight = targets
    copies = fetch(sources, targets, arrived)
    col, row = place[0], place[1]
    seqs, own, channels = alignment.shape
    total = cotangent.shape[1]
    depth = Z // count
    half = LANES // 2
    pairs = own // 2
    for k in range(count):
        peer = col ^ k
        at = pl.multiple_of(peer * own, own)
        message = messages[k]
        block = message[0:PROJ_ROWS, :].astype(F32)
        for q in range(P_SIZE):
            every[pl.ds(q * total + at, own), :] = block[q * own : (q + 1) * own]
        masks = message[MASK_AT:TURNED_AT, :].astype(F32)
        live_all[pl.ds(at, own), :] = masks[:own]
        present_all[pl.ds(at, own), :] = masks[own:]
        block = message[TURNED_AT:SLICE_AT, :].astype(F32)
        for j in range(own):
            turned[pl.ds(j * total + at, own), :] = block[j * own : (j + 1) * own]
        slices[peer] = message[SLICE_AT:MESSAGE, :]
    live = live_all[...].astype(BF16)
    present = present_all[...].astype(BF16)
    masks = messages[0][MASK_AT:TURNED_AT, :]
    live_own = masks[:own].astype(F32)
    present_own = masks[own:]

    def scale_of(live_other, present_other):
        counts = dot_nt(live, live_other)
        return dot_nt(present, present_other) * (1.0 / LANES) / jnp.maximum(counts, 1.0)

    scale_own = scale_of(masks[:own], present_own)
    scale_twice = scale_of(
        jnp.concatenate([live, live], axis=0), jnp.concatenate([present, present], axis=0)
    )
    copies[0].wait()
    for i in range(own):
        rows = slice(i * total, (i + 1) * total)
        grad_own[rows, :] = (cotangent[i].astype(F32) * scale_own[:, i : i + 1]).astype(BF16)
        grad_turned[rows, :] = (turned[rows, :] * scale_own[:, i : i + 1]).astype(BF16)
    low = low_lanes((own, LANES))
    bias_acc = jnp.zeros((depth, LANES), F32)
    for c in range(count):
        tile = scale_twice[c * own : (c + 1) * own]
        tile = jnp.where(low, tile, jnp.concatenate([tile[pairs:], tile[:pairs]], axis=0))
        for i in range(pairs):
            piece = slices[c, i * depth : (i + 1) * depth, :].astype(F32) * tile[i : i + 1, :]
            bias_acc = bias_acc + piece
            grad_slice[
                (c * 2 + i // 2) * depth : (c * 2 + i // 2 + 1) * depth,
                i % 2 * LANES : (i % 2 + 1) * LANES,
            ] = piece.astype(BF16)

    copies[1].wait()
    wide[0] = out_weight[...].astype(F32)
    eight = 8
    for a in range(0, P_SIZE, eight):
        rows = slice(a * P_SIZE, (a + eight) * P_SIZE)
        by_second = jnp.concatenate(
            [wide[0, pl.ds(q, P_SIZE, stride=P_SIZE), :] for q in range(a, a + eight)], axis=0
        ).astype(BF16)
        interleave(dot_nt(by_second, grad_own[...]), left_outer, own, a)
        interleave(dot_nt(out_weight[rows, :], grad_turned[...]), right_outer, own, a)
    gathered = every[...].astype(BF16)
    left_grad = swap_halves(dot_nn(left_outer[...], gathered))
    right_grad = dot_nn(right_outer[...], gathered)

    for copy in copies[2:]:
        copy.wait()
    square = wide.at[0, 0:LANES, :]
    stats = columns_of(square, [mean[...], inverse[...]])
    spread(wide, alignment)
    input_acc = jnp.zeros((2 * P_SIZE, channels), F32)
    proj_acc = jnp.zeros((2 * P_SIZE, seqs), F32)
    gain_acc = jnp.zeros((1, channels), F32)
    shift_acc = jnp.zeros((1, channels), F32)
    for r in range(own):
        spot = pl.ds(r, seqs, stride=own)
        scale = stats[:seqs, own + r : own + r + 1]
        hatted = (strided(wide, r, seqs, own) - stats[:seqs, r : r + 1]) * scale
        normed = (hatted * gain[...] + shift[...]).astype(BF16)
        rows = slice(r * P_SIZE, (r + 1) * P_SIZE)
        proj_grad = jnp.concatenate([left_grad[rows, :seqs], right_grad[rows, :seqs]], axis=0)
        proj_grad = proj_grad * live_own[r : r + 1, :seqs]
        proj_acc = proj_acc + proj_grad
        input_acc = input_acc + dot_nn(proj_grad.astype(BF16), normed)
        normed_grad = dot_nn(proj_grad.T.astype(BF16), weight[...])
        gain_acc = gain_acc + jnp.sum(normed_grad * hatted, axis=0, keepdims=True)
        shift_acc = shift_acc + jnp.sum(normed_grad, axis=0, keepdims=True)
        hat_grad = normed_grad * gain[...]
        first = jnp.sum(hat_grad, axis=1, keepdims=True) * (1.0 / channels)
        second = jnp.sum(hat_grad * hatted, axis=1, keepdims=True) * (1.0 / channels)
        result = scale * (hat_grad - first - hatted * second)
        for h in range(2):
            wide[h, spot, :] = result[:, h * LANES : (h + 1) * LANES]
    activation[...] = jnp.concatenate(
        [wide[h, 0 : seqs * own, :].reshape(seqs, own, LANES) for h in range(2)], axis=2
    ).astype(BF16)

    quads = count * own // 4
    span = quads * depth
    low = low_lanes((total, LANES))
    corner[...] = jnp.zeros_like(corner)
    for q in range(P_SIZE):
        block = every[q * total : (q + 1) * total, :]
        here = jnp.where(low, 0.0, block)
        moved = swap_halves(here).astype(BF16)
        here = here.astype(BF16)
        slot = q % corner.shape[0]
        for at in range(4):
            lanes = slice(at // 2 * LANES, (at // 2 + 1) * LANES)
            corner[slot, at * total : (at + 1) * total, lanes] = here if at % 2 else moved
        mixed[:, q * depth : (q + 1) * depth, :] = (
            dot_nn(grad_slice[...], corner[slot]).astype(BF16).reshape(quads, depth, 4 * total)
        )
    low = low_lanes((P_SIZE, LANES))
    weight_acc = jnp.zeros((P_SIZE * depth, P_SIZE), F32)
    for quad in range(quads):
        rhs = []
        for first in quad_members(quad):
            one, two = (every[pl.ds(i, P_SIZE, stride=total), :] for i in first)
            rhs.append(jnp.where(low, one, swap_halves(two)))
        weight_acc = weight_acc + dot_nt(mixed[quad], jnp.concatenate(rhs, axis=1).astype(BF16))
    group = P_SIZE * depth // 4
    weight_acc = jnp.concatenate([weight_acc[b * group : (b + 1) * group] for b in range(4)], axis=1)

    square[...] = jnp.zeros((LANES, LANES), F32)
    square[0 : 2 * P_SIZE, :seqs] = proj_acc
    square[half : half + depth, :] = bias_acc
    sums = jnp.sum(square[...].T, axis=0, keepdims=True)
    lane = lax.broadcasted_iota(jnp.int32, (1, LANES), 1)
    small = [gain_acc[:, :LANES], gain_acc[:, LANES:], shift_acc[:, :LANES], shift_acc[:, LANES:]]
    none = jnp.zeros((3, LANES), F32)
    first = row == 0
    keep[0:half, :] = jnp.where(first, weight_acc[:half], weight_acc[half:])
    give[0:half, :] = jnp.where(first, weight_acc[half:], weight_acc[:half])
    keep[half:LANES, :] = jnp.where(first, input_acc[:, :LANES], input_acc[:, LANES:])
    give[half:LANES, :] = jnp.where(first, input_acc[:, LANES:], input_acc[:, :LANES])
    keep[LANES:PARTIAL, :] = jnp.concatenate(small + [sums, none], axis=0)
    give[LANES:PARTIAL, :] = jnp.concatenate(small + [jnp.where(lane < half, sums, 0.0), none], axis=0)


def pack(kept, given, partial):
    both = kept[...] + given[...]
    high = both.astype(BF16)
    small = both[LANES:] - high[LANES:].astype(F32)
    whole = jnp.concatenate([high, small.astype(BF16)], axis=0)
    for k in range(partial.shape[0]):
        partial[k] = whole


def finish(place, own, mate, input_out, bias_out, weight_out, out_bias_out, gain_out, shift_out):
    row = place[1]
    count = own.shape[0]
    depth = Z // count
    half = LANES // 2
    lane = lax.broadcasted_iota(jnp.int32, (1, LANES), 1)
    sums = []
    for side, part in enumerate((own, mate)):
        top = row if side == 0 else 1 - row
        input_acc = jnp.zeros((half, LANES), F32)
        pieces = []
        for k in range(count):
            pieces.append(part[k, :half].astype(F32))
            input_acc = input_acc + part[k, half:LANES].astype(F32)
        sums.append(input_acc)
        for a in range(4):
            turned = jnp.concatenate([p[a * depth : (a + 1) * depth] for p in pieces], axis=0).T
            for b in range(4):
                weight_out[pl.ds(4 * top + a + 8 * b, P_SIZE, stride=P_SIZE), :] = turned[
                    b * P_SIZE : (b + 1) * P_SIZE
                ]
    input_out[:, :LANES] = jnp.where(row == 0, sums[0], sums[1])
    input_out[:, LANES:] = jnp.where(row == 0, sums[1], sums[0])
    small_acc = jnp.zeros((8, LANES), F32)
    out_bias = jnp.zeros((1, LANES), F32)
    for k in range(count):
        small = part_of_small(own, k)
        small_acc = small_acc + small
        bias = pltpu.roll(small[4:5], (k * depth + half) % LANES, 1)
        out_bias = jnp.where((lane >= k * depth) & (lane < (k + 1) * depth), bias, out_bias)
    gain_out[:, :LANES] = small_acc[0:1]
    gain_out[:, LANES:] = small_acc[1:2]
    shift_out[:, :LANES] = small_acc[2:3]
    shift_out[:, LANES:] = small_acc[3:4]
    bias_out[...] = small_acc[4:5, :half]
    out_bias_out[...] = out_bias


def part_of_small(own, k):
    both = own[k, LANES:].astype(F32)
    return both[:8] + both[8:]


def shape(dims, dtype):
    return jax.ShapeDtypeStruct(dims, dtype)


def tiled(
    alignment,
    norm_mean,
    norm_inverse,
    norm_gain,
    norm_shift,
    input_weight,
    input_bias,
    output_weight,
    pair_cotangent,
    residue_mask,
    sequence_mask,
):
    count = lax.axis_size("col")
    seqs, own, channels = alignment.shape
    total = pair_cotangent.shape[1]
    place = jnp.stack([lax.axis_index("col"), lax.axis_index("row")]).astype(jnp.int32)
    mask = sequence_mask.T
    turn = [(0, 1), (1, 0)]
    mate = lax.ppermute(mask, "row", turn)
    mean, inverse = norm_mean.T, norm_inverse.T
    gain, shift = norm_gain[None, :], norm_shift[None, :]
    weight = input_weight.T
    smem = pl.BlockSpec(memory_space=pltpu.SMEM)
    vmem = pl.BlockSpec(memory_space=pltpu.VMEM)
    hbm = pl.BlockSpec(memory_space=pltpu.HBM)

    def room(arrays):
        return [pltpu.VMEM(a.shape, a.dtype) for a in arrays]

    def stay(arrays):
        return [pltpu.with_memory_space_constraint(a, pltpu.HBM) for a in arrays]

    operands = [alignment, mean, inverse, gain, shift, weight, input_bias[None, :], mask, pair_cotangent]
    messages = pl.pallas_call(
        prepare,
        out_shape=[shape((MESSAGE, LANES), BF16)] * count,
        in_specs=[smem, smem, vmem] + [hbm] * len(operands),
        out_specs=[vmem] * count,
        scratch_shapes=room(operands)
        + [
            pltpu.VMEM((2, seqs * own, LANES), F32),
            pltpu.VMEM((PROJ_ROWS, LANES), F32),
            pltpu.VMEM((own * total, Z), F32),
            pltpu.VMEM((own // 2, Z, LANES), BF16),
            pltpu.SemaphoreType.DMA((len(operands),)),
        ],
        compiler_params=VMEM,
        name="prepare",
    )(place, stay([residue_mask])[0], mate, *stay(operands))
    received = [messages[0]] + [
        lax.ppermute(messages[k], "col", [(c, c ^ k) for c in range(count)]) for k in range(1, count)
    ]
    operands = [pair_cotangent, output_weight, alignment, mean, inverse, gain, shift, weight]
    activation, keep, give = pl.pallas_call(
        work,
        out_shape=[shape(alignment.shape, BF16)] + [shape((PARTIAL, LANES), F32)] * 2,
        in_specs=[smem] + [vmem] * count + [hbm] * len(operands),
        out_specs=[vmem] * 3,
        scratch_shapes=room(operands)
        + [
            pltpu.VMEM((P_SIZE * total, LANES), F32),
            pltpu.VMEM((total, LANES), F32),
            pltpu.VMEM((total, LANES), F32),
            pltpu.VMEM((own * total, Z), F32),
            pltpu.VMEM((count, MESSAGE - SLICE_AT, LANES), BF16),
            pltpu.VMEM((own * total, Z), BF16),
            pltpu.VMEM((own * total, Z), BF16),
            pltpu.VMEM((count * (MESSAGE - SLICE_AT) // 2, 2 * LANES), BF16),
            pltpu.VMEM((own * P_SIZE, P_SIZE * total), BF16),
            pltpu.VMEM((own * P_SIZE, P_SIZE * total), BF16),
            pltpu.VMEM((4, 4 * total, 2 * LANES), BF16),
            pltpu.VMEM((count * own // 4, P_SIZE * (Z // count), 4 * seqs), BF16),
            pltpu.VMEM((2, P_SIZE * P_SIZE, LANES), F32),
            pltpu.SemaphoreType.DMA((len(operands),)),
        ],
        compiler_params=VMEM,
        name="work",
    )(place, *received, *stay(operands))
    partial = pl.pallas_call(
        pack,
        out_shape=shape((count, SENT, LANES), BF16),
        in_specs=[vmem] * 2,
        out_specs=vmem,
        compiler_params=VMEM,
        name="pack",
    )(keep, lax.ppermute(give, "row", turn))
    ours = lax.all_to_all(partial, "col", 0, 0)
    theirs = lax.ppermute(ours, "row", turn)
    input_grad, bias_grad, weight_grad, out_bias_grad, gain_grad, shift_grad = pl.pallas_call(
        finish,
        out_shape=[
            shape((2 * P_SIZE, channels), F32),
            shape((1, 2 * P_SIZE), F32),
            shape((P_SIZE * P_SIZE, Z), F32),
            shape((1, Z), F32),
            shape((1, channels), F32),
            shape((1, channels), F32),
        ],
        in_specs=[smem] + [vmem] * 2,
        out_specs=[vmem] * 6,
        compiler_params=VMEM,
        name="finish",
    )(place, ours, theirs)
    return (activation, input_grad.T, bias_grad[0], weight_grad, out_bias_grad[0], gain_grad[0], shift_grad[0])


def local(*args):
    alignment, cotangent = args[0], args[8]
    seqs, own, channels = alignment.shape
    total = cotangent.shape[1]
    count = lax.axis_size("col")
    fits = (
        2 * seqs == LANES
        and 2 * total == LANES
        and own == 8
        and channels == 2 * LANES
        and count == 8
        and lax.axis_size("row") == 2
    )
    return tiled(*args) if fits else general(*args)


def solution(mesh):
    in_specs = (
        P(("group", "row"), "col", None),
        P(("group", "row"), "col"),
        P(("group", "row"), "col"),
        P(),
        P(),
        P(),
        P(),
        P(),
        P("col", "group", None),
        P("group"),
        P(("group", "row"), "col"),
    )
    out_specs = (
        P(("group", "row"), "col", None),
        P("group", None),
        P("group"),
        P("group", None),
        P("group"),
        P("group"),
        P("group"),
    )
    return jax.shard_map(local, mesh=mesh, in_specs=in_specs, out_specs=out_specs, check_vma=False)
```

```python
import math

import jax
import jax.numpy as jnp
from jax import lax
from jax.experimental import pallas as pl
from jax.experimental.pallas import tpu as pltpu
from jax.sharding import PartitionSpec as P

C = 256
P_SIZE = 32
Z = 128


def normalize(alignment, norm_mean, norm_inverse, norm_gain, norm_shift):
    hatted = (alignment.astype(jnp.float32) - norm_mean[..., None]) * norm_inverse[..., None]
    normed = (hatted * norm_gain + norm_shift).astype(jnp.bfloat16)
    return (hatted, normed)


def project(normed, input_weight, input_bias, live):
    flat = normed.reshape(-1, normed.shape[-1])
    projected = jnp.dot(flat, input_weight, preferred_element_type=jnp.float32) + input_bias
    projected = projected.reshape(normed.shape[:-1] + (input_weight.shape[1],)) * live[..., None]
    return projected.astype(jnp.bfloat16)


def contract(left, right, counts, cotangent, pair_live, output_weight):
    sequence_count, row_count, _ = left.shape
    column_total = right.shape[1]
    width = math.gcd(column_total, 128)
    left_acc = jnp.zeros(left.shape, jnp.float32)
    weight_acc = jnp.zeros((P_SIZE * P_SIZE, Z), jnp.float32)
    bias_acc = jnp.zeros((Z,), jnp.float32)
    pieces = []
    for offset in range(0, column_total, width):
        right_cols = right[:, offset : offset + width]
        scale = pair_live[:, offset : offset + width] / jnp.maximum(
            counts[:, offset : offset + width], 1.0
        )
        pair_grad = cotangent[:, offset : offset + width].astype(jnp.float32) * scale[..., None]
        pair_low = pair_grad.astype(jnp.bfloat16).reshape(-1, Z)
        outer_grad = jnp.einsum(
            "ne,ke->nk", pair_low, output_weight, preferred_element_type=jnp.float32
        )
        outer_grad = outer_grad.astype(jnp.bfloat16).reshape(row_count, width, P_SIZE, P_SIZE)
        left_acc = left_acc + jnp.einsum(
            "ijpq,sjq->sip", outer_grad, right_cols, preferred_element_type=jnp.float32
        )
        pieces.append(
            jnp.einsum("ijpq,sip->sjq", outer_grad, left, preferred_element_type=jnp.float32)
        )
        outer = jnp.einsum(
            "sip,sjq->ijpq", left, right_cols, preferred_element_type=jnp.float32
        ).reshape(-1, P_SIZE * P_SIZE)
        outer_high = outer.astype(jnp.bfloat16)
        outer_rest = (outer - outer_high.astype(jnp.float32)).astype(jnp.bfloat16)
        weight_acc = weight_acc + jnp.einsum(
            "nk,ne->ke", outer_high, pair_low, preferred_element_type=jnp.float32
        )
        weight_acc = weight_acc + jnp.einsum(
            "nk,ne->ke", outer_rest, pair_low, preferred_element_type=jnp.float32
        )
        bias_acc = bias_acc + jnp.sum(pair_grad, axis=(0, 1))
    right_out = jnp.concatenate(pieces, axis=1)
    return (left_acc, right_out, weight_acc, bias_acc)


def general(
    alignment,
    norm_mean,
    norm_inverse,
    norm_gain,
    norm_shift,
    input_weight,
    input_bias,
    output_weight,
    pair_cotangent,
    residue_mask,
    sequence_mask,
):
    sequence_count, residue_count = sequence_mask.shape
    residue_total = residue_mask.shape[0]
    column = lax.axis_index("col")
    residue_float = residue_mask.astype(jnp.float32)
    own_residues = lax.dynamic_slice_in_dim(residue_float, column * residue_count, residue_count, 0)
    own_mask = lax.dynamic_slice_in_dim(residue_mask, column * residue_count, residue_count, 0)
    live_int = sequence_mask * own_mask[None, :]
    live = live_int.astype(jnp.float32)
    hatted, normed = normalize(alignment, norm_mean, norm_inverse, norm_gain, norm_shift)
    projected = project(normed, input_weight, input_bias, live)
    left = projected[..., :P_SIZE]
    right = projected[..., P_SIZE:]
    gathered, mask_cols = (
        lax.all_gather(
            right.reshape(sequence_count, residue_count * P_SIZE), "col", axis=1, tiled=True
        ),
        lax.all_gather(live_int, "col", axis=1, tiled=True),
    )
    right_all = gathered.reshape(sequence_count, residue_total, P_SIZE)
    partial_counts = jnp.dot(live.T, mask_cols.astype(jnp.float32), precision=lax.Precision.HIGHEST)
    counts = lax.psum(partial_counts, "row")
    pair_live = own_residues[:, None] * residue_float[None, :]
    left_grad, right_part, weight_out, bias_out = contract(
        left, right_all, counts, pair_cotangent, pair_live, output_weight
    )
    bias_out = bias_out / lax.axis_size("row")
    summed = lax.psum_scatter(
        right_part.reshape(sequence_count, residue_total * P_SIZE),
        "col",
        scatter_dimension=1,
        tiled=True,
    )
    right_grad = summed.reshape(sequence_count, residue_count, P_SIZE)
    proj_grad = jnp.concatenate([left_grad, right_grad], axis=-1) * live[..., None]
    proj_low = proj_grad.astype(jnp.bfloat16).reshape(-1, 2 * P_SIZE)
    flat_normed = normed.reshape(-1, C)
    weight_part = jnp.einsum("nc,nk->ck", flat_normed, proj_low, preferred_element_type=jnp.float32)
    bias_part = jnp.sum(proj_grad, axis=(0, 1))
    normed_grad = jnp.einsum(
        "nk,ck->nc", proj_low, input_weight, preferred_element_type=jnp.float32
    ).reshape(hatted.shape)
    gain_part = jnp.sum(normed_grad * hatted, axis=(0, 1))
    shift_part = jnp.sum(normed_grad, axis=(0, 1))
    hat_grad = normed_grad * norm_gain
    centered = (
        hat_grad
        - jnp.mean(hat_grad, axis=-1, keepdims=True)
        - hatted * jnp.mean(hat_grad * hatted, axis=-1, keepdims=True)
    )
    activation_grad = (norm_inverse[..., None] * centered).astype(jnp.bfloat16)
    totals = lax.psum(
        (weight_part, bias_part, gain_part, shift_part, weight_out, bias_out), ("row", "col")
    )
    return (activation_grad, totals[0], totals[1], totals[4], totals[5], totals[2], totals[3])


LANES = 128
PROJ_ROWS = 256
MASK_AT = 256
COT_AT = 272
MESSAGE = 336
SMALL_AT = 256
PARTIAL = 264
SENT = 272
PEERS = ((4, 5, 1, 0), (6, 7, 2, 3))
ORDER = (0, 4, 1, 5, 6, 2, 7, 3)
VMEM = pltpu.CompilerParams(vmem_limit_bytes=24 * 1024 * 1024)
F32 = jnp.float32
BF16 = jnp.bfloat16


def dot_nt(a, b):
    return lax.dot_general(a, b, (((1,), (1,)), ((), ())), preferred_element_type=F32)


def dot_nn(a, b):
    return lax.dot_general(a, b, (((1,), (0,)), ((), ())), preferred_element_type=F32)


def low_lanes(shape):
    return lax.broadcasted_iota(jnp.int32, shape, 1) < LANES // 2


def swap_halves(x):
    return pltpu.roll(x, LANES // 2, 1)


def strided(wide, start, size, stride):
    return jnp.concatenate([wide[h, pl.ds(start, size, stride=stride), :] for h in range(2)], axis=1)


def prepare(*rest):
    sources = rest[:11]
    mask, gain, shift, weight, cotangent, out_weight, hat, stats, present = rest[11:20]
    messages = rest[20:-12]
    count = len(messages)
    alignment, mean, inverse, bias, residue, wide, packed, cot, turned, square, arrived, late = rest[-12:]
    targets = (alignment, mean, inverse, bias, residue, mask, gain, shift, weight, cotangent)
    copies = [pltpu.make_async_copy(f, t, arrived.at[i]) for i, (f, t) in enumerate(zip(sources, targets))]
    for copy in copies:
        copy.start()
    last = pltpu.make_async_copy(sources[-1], out_weight, late)
    last.start()
    for copy in copies:
        copy.wait()
    col, row = lax.axis_index("col"), lax.axis_index("row")
    seqs, own, channels = alignment.shape
    total = cotangent.shape[1]
    square[0:own, :seqs] = mean[...]
    square[own : 2 * own, :seqs] = inverse[...]
    square[2 * own : 3 * own, : 2 * P_SIZE] = jnp.broadcast_to(bias[...], (own, 2 * P_SIZE))
    square[3 * own : 4 * own, :total] = jnp.broadcast_to(residue[...].astype(F32), (own, total))
    stats[...] = square[...].T
    own_rows = pl.ds(pl.multiple_of(col * own, own), own)
    present[...] = jnp.broadcast_to(stats[own_rows, 3 * own : 3 * own + 1], (own, LANES))
    live = mask[...].astype(F32) * present[:, :seqs]
    values = alignment[...].astype(F32)
    for h in range(2):
        wide[h] = values[:, :, h * LANES : (h + 1) * LANES].reshape(seqs * own, LANES)
    for r in range(own):
        hatted = (strided(wide, r, seqs, own) - stats[:seqs, r : r + 1]) * stats[
            :seqs, own + r : own + r + 1
        ]
        hat[r] = hatted
        normed = (hatted * gain[...] + shift[...]).astype(BF16)
        projected = dot_nt(weight[...], normed) + stats[: 2 * P_SIZE, 2 * own : 2 * own + 1]
        projected = projected * live[r : r + 1]
        packed[pl.ds(r, P_SIZE, stride=own), :] = jnp.concatenate(
            [projected[:P_SIZE], projected[P_SIZE:]], axis=1
        )
    shared = packed[...].astype(BF16)
    depth = Z // count
    for message in messages:
        message[0:PROJ_ROWS, :] = shared

    @pl.when(row == 0)
    def _():
        cot[...] = cotangent[...].astype(F32).reshape(own * total, Z)
        for k, message in enumerate(messages):
            peer = col ^ ORDER[k]
            message[COT_AT:MESSAGE, :] = jnp.concatenate(
                [cot[pl.ds(own * peer + j, own, stride=total), :] for j in range(own)], axis=0
            ).astype(BF16)

    @pl.when(row != 0)
    def _():
        for i in range(own // 2):
            pair = jnp.concatenate([cotangent[i], cotangent[i + own // 2]], axis=0).astype(F32)
            turned[i] = pair.T.astype(BF16)
        for k, message in enumerate(messages):
            at = pl.multiple_of((col ^ ORDER[k]) * depth, depth)
            for i in range(own // 2):
                message[COT_AT + i * depth : COT_AT + (i + 1) * depth, :] = turned[i, pl.ds(at, depth), :]

    last.wait()


def add_masks(mask, present, mate, *rest):
    messages = rest[len(rest) // 2 :]
    here = present[...]
    live = jnp.concatenate([mask[...], mate[...]], axis=1).astype(F32) * here
    masks = jnp.concatenate([live, here], axis=0).astype(BF16)
    for message in messages:
        message[MASK_AT:COT_AT, :] = masks


def collect(*rest):
    messages, cots = rest[:-1], rest[-1]
    col = lax.axis_index("col")
    for k, message in enumerate(messages):
        cots[col ^ ORDER[k]] = message[COT_AT:MESSAGE, :]


def interleave(product, target, group, at):
    half = LANES // 2
    low = low_lanes((P_SIZE, LANES))
    for a in range(0, product.shape[0] // P_SIZE, 2):
        for b in range(0, group, 2):
            first = product[a * P_SIZE : (a + 1) * P_SIZE, b * half : (b + 2) * half]
            second = product[(a + 1) * P_SIZE : (a + 2) * P_SIZE, b * half : (b + 2) * half]
            lanes = slice((at + a) * half, (at + a + 2) * half)
            target[b * P_SIZE : (b + 1) * P_SIZE, lanes] = jnp.where(
                low, first, swap_halves(second)
            ).astype(BF16)
            target[(b + 1) * P_SIZE : (b + 2) * P_SIZE, lanes] = jnp.where(
                low, swap_halves(first), second
            ).astype(BF16)


BLOCK = 8


def left_part(cotangent, out_weight, *rest):
    messages = rest[:-11]
    every, gathered, scale_own, scale_twice, live_out, left_grad, live_all, present_all, grad_own, outer, wide = rest[-11:]
    col = lax.axis_index("col")
    own, total = cotangent.shape[:2]
    for k, message in enumerate(messages):
        at = pl.multiple_of((col ^ ORDER[k]) * own, own)
        block = message[0:PROJ_ROWS, :].astype(F32)
        for q in range(P_SIZE):
            every[pl.ds(q * total + at, own), :] = block[q * own : (q + 1) * own]
        masks = message[MASK_AT:COT_AT, :].astype(F32)
        live_all[pl.ds(at, own), :] = masks[:own]
        present_all[pl.ds(at, own), :] = masks[own:]
    live = live_all[...].astype(BF16)
    present = present_all[...].astype(BF16)
    masks = messages[0][MASK_AT:COT_AT, :]
    live_out[...] = masks[:own].astype(F32)

    def scale_of(live_other, present_other):
        counts = dot_nt(live, live_other)
        return dot_nt(present, present_other) * (1.0 / LANES) / jnp.maximum(counts, 1.0)

    scale_own[:, :own] = scale_of(masks[:own], masks[own:])
    scale_twice[...] = scale_of(
        jnp.concatenate([live, live], axis=0), jnp.concatenate([present, present], axis=0)
    )
    for i in range(own):
        grad_own[i * total : (i + 1) * total, :] = (
            cotangent[i].astype(F32) * scale_own[:, i : i + 1]
        ).astype(BF16)
    wide[...] = out_weight[...].astype(F32)
    for a in range(0, P_SIZE, BLOCK):
        by_second = jnp.concatenate(
            [wide[pl.ds(q, P_SIZE, stride=P_SIZE), :] for q in range(a, a + BLOCK)], axis=0
        ).astype(BF16)
        interleave(dot_nt(by_second, grad_own[...]), outer, own, a)
    gathered[...] = every[...].astype(BF16)
    left_grad[...] = swap_halves(dot_nn(outer[...], gathered[...]))


def quad_members(quad):
    base = quad // 2 * 8 + quad % 2 * 2
    return ((base, base + 4), (base + 1, base + 5))


def sums_part(
    cots, mate, out_weight, every, gathered, scale_own, scale_twice, live, left_grad, hat, gain, shift, weight, normed_grads, keep, turned, grad_turned, grad_slice, outer, corner, mixed, square
):
    row = lax.axis_index("row")
    count = cots.shape[0]
    own, seqs, channels = hat.shape
    total = grad_turned.shape[0] // own
    depth = Z // count
    half = LANES // 2
    pairs = own // 2
    mine = row == 0
    low = low_lanes((own, LANES))
    bias_acc = jnp.zeros((depth, LANES), F32)
    for c in range(count):
        one, two = cots[c].astype(F32), mate[c].astype(F32)
        block = jnp.where(mine, one, two)
        for j in range(own):
            turned[j * total + c * own : j * total + (c + 1) * own, :] = block[j * own : (j + 1) * own]
        block = jnp.where(mine, two, one)
        tile = scale_twice[c * own : (c + 1) * own, :]
        tile = jnp.where(low, tile, jnp.concatenate([tile[pairs:], tile[:pairs]], axis=0))
        for i in range(pairs):
            piece = block[i * depth : (i + 1) * depth] * tile[i : i + 1, :]
            bias_acc = bias_acc + piece
            grad_slice[
                (c * 2 + i // 2) * depth : (c * 2 + i // 2 + 1) * depth,
                i % 2 * LANES : (i % 2 + 1) * LANES,
            ] = piece.astype(BF16)
    for j in range(own):
        spot = slice(j * total, (j + 1) * total)
        grad_turned[spot, :] = (turned[spot, :] * scale_own[:, j : j + 1]).astype(BF16)
    for a in range(0, P_SIZE, BLOCK):
        interleave(
            dot_nt(out_weight[a * P_SIZE : (a + BLOCK) * P_SIZE, :], grad_turned[...]), outer, own, a
        )
    right_grad = dot_nn(outer[...], gathered[...])

    input_acc = jnp.zeros((2 * P_SIZE, channels), F32)
    proj_acc = jnp.zeros((2 * P_SIZE, seqs), F32)
    gain_acc = jnp.zeros((1, channels), F32)
    shift_acc = jnp.zeros((1, channels), F32)
    for r in range(own):
        hatted = hat[r]
        normed = (hatted * gain[...] + shift[...]).astype(BF16)
        spot = slice(r * P_SIZE, (r + 1) * P_SIZE)
        proj_grad = jnp.concatenate([left_grad[spot, :seqs], right_grad[spot, :seqs]], axis=0)
        proj_grad = proj_grad * live[r : r + 1, :seqs]
        proj_acc = proj_acc + proj_grad
        input_acc = input_acc + dot_nn(proj_grad.astype(BF16), normed)
        normed_grad = dot_nn(proj_grad.T.astype(BF16), weight[...])
        gain_acc = gain_acc + jnp.sum(normed_grad * hatted, axis=0, keepdims=True)
        shift_acc = shift_acc + jnp.sum(normed_grad, axis=0, keepdims=True)
        normed_grads[r] = normed_grad

    quads = count * own // 4
    low = low_lanes((total, LANES))
    corner[...] = jnp.zeros_like(corner)
    for q in range(P_SIZE):
        block = every[q * total : (q + 1) * total, :]
        here = jnp.where(low, 0.0, block)
        moved = swap_halves(here).astype(BF16)
        here = here.astype(BF16)
        slot = q % corner.shape[0]
        for at in range(4):
            lanes = slice(at // 2 * LANES, (at // 2 + 1) * LANES)
            corner[slot, at * total : (at + 1) * total, lanes] = here if at % 2 else moved
        mixed[:, q * depth : (q + 1) * depth, :] = (
            dot_nn(grad_slice[...], corner[slot]).astype(BF16).reshape(quads, depth, 4 * total)
        )
    low = low_lanes((P_SIZE, LANES))
    weight_acc = jnp.zeros((P_SIZE * depth, P_SIZE), F32)
    for quad in range(quads):
        rhs = []
        for pair in quad_members(quad):
            one, two = (every[pl.ds(i, P_SIZE, stride=total), :] for i in pair)
            rhs.append(jnp.where(low, one, swap_halves(two)))
        weight_acc = weight_acc + dot_nt(mixed[quad], jnp.concatenate(rhs, axis=1).astype(BF16))
    group = P_SIZE * depth // 4
    weight_acc = jnp.concatenate([weight_acc[b * group : (b + 1) * group] for b in range(4)], axis=1)

    square[...] = jnp.zeros((LANES, LANES), F32)
    square[0 : 2 * P_SIZE, :seqs] = proj_acc
    square[half : half + depth, :] = bias_acc * 0.5
    sums = jnp.sum(square[...].T, axis=0, keepdims=True)
    keep[0:LANES, :] = weight_acc
    for h in range(2):
        lanes = slice(h * LANES, (h + 1) * LANES)
        keep[LANES + h * half : LANES + (h + 1) * half, :] = input_acc[:, lanes]
        keep[SMALL_AT + h : SMALL_AT + h + 1, :] = gain_acc[:, lanes]
        keep[SMALL_AT + 2 + h : SMALL_AT + 3 + h, :] = shift_acc[:, lanes]
    keep[SMALL_AT + 4 : PARTIAL, :] = jnp.concatenate([sums, jnp.zeros((3, LANES), F32)], axis=0)


def activations(normed_grads, hat, stats, gain, activation, wide):
    own, seqs, channels = hat.shape
    for r in range(own):
        hatted = hat[r]
        hat_grad = normed_grads[r] * gain[...]
        first = jnp.sum(hat_grad, axis=1, keepdims=True) * (1.0 / channels)
        second = jnp.sum(hat_grad * hatted, axis=1, keepdims=True) * (1.0 / channels)
        result = stats[:seqs, own + r : own + r + 1] * (hat_grad - first - hatted * second)
        for h in range(2):
            wide[h, pl.ds(r, seqs, stride=own), :] = result[:, h * LANES : (h + 1) * LANES]
    activation[...] = jnp.concatenate(
        [wide[h].reshape(seqs, own, LANES) for h in range(2)], axis=2
    ).astype(BF16)


def pack(kept, given, partial):
    both = kept[...] + given[...]
    high = both.astype(BF16)
    small = both[SMALL_AT:] - high[SMALL_AT:].astype(F32)
    partial[...] = jnp.concatenate([high, small.astype(BF16)], axis=0)


def stack(*rest):
    for k, part in enumerate(rest[:-1]):
        rest[-1][k] = part[...]


def finish(own, received, mate, input_out, bias_out, weight_out, out_bias_out, gain_out, shift_out, ordered):
    col, row = lax.axis_index("col"), lax.axis_index("row")
    count = ordered.shape[0]
    depth = Z // count
    half = LANES // 2
    lane = lax.broadcasted_iota(jnp.int32, (1, LANES), 1)
    ordered[col] = own[...]
    for k, (one, two) in enumerate(zip(*PEERS)):
        ordered[col ^ jnp.where(row == 0, one, two)] = received[k]
        ordered[col ^ jnp.where(row == 0, two, one)] = mate[k]
    ordered[col] = own[...]
    for a in range(8):
        turned = jnp.concatenate(
            [ordered[c, a * depth : (a + 1) * depth] for c in range(count)], axis=0
        ).astype(F32).T
        for b in range(4):
            weight_out[pl.ds(8 * b + a, P_SIZE, stride=P_SIZE), :] = turned[b * P_SIZE : (b + 1) * P_SIZE]
    input_acc = jnp.zeros((LANES, LANES), F32)
    small_acc = jnp.zeros((8, LANES), F32)
    out_bias = jnp.zeros((1, LANES), F32)
    for c in range(count):
        input_acc = input_acc + ordered[c, LANES:SMALL_AT].astype(F32)
        both = ordered[c, SMALL_AT:].astype(F32)
        small = both[:8] + both[8:]
        small_acc = small_acc + small
        bias = pltpu.roll(small[4:5], (c * depth + half) % LANES, 1)
        out_bias = jnp.where((lane >= c * depth) & (lane < (c + 1) * depth), bias, out_bias)
    for h in range(2):
        lanes = slice(h * LANES, (h + 1) * LANES)
        input_out[:, lanes] = input_acc[h * half : (h + 1) * half]
        gain_out[:, lanes] = small_acc[h : h + 1]
        shift_out[:, lanes] = small_acc[2 + h : 3 + h]
    bias_out[...] = small_acc[4:5, :half]
    out_bias_out[...] = out_bias


def shape(dims, dtype):
    return jax.ShapeDtypeStruct(dims, dtype)


VMEM_SPEC = pl.BlockSpec(memory_space=pltpu.VMEM)
HBM_SPEC = pl.BlockSpec(memory_space=pltpu.HBM)


def call(kernel, outputs, specs, arguments, scratch=(), aliases=None):
    return pl.pallas_call(
        kernel,
        out_shape=outputs,
        in_specs=specs,
        out_specs=[VMEM_SPEC] * len(outputs),
        scratch_shapes=list(scratch),
        input_output_aliases=aliases or {},
        compiler_params=VMEM,
        name=kernel.__name__,
    )(*arguments)


def tiled(
    alignment,
    norm_mean,
    norm_inverse,
    norm_gain,
    norm_shift,
    input_weight,
    input_bias,
    output_weight,
    pair_cotangent,
    residue_mask,
    sequence_mask,
):
    count = lax.axis_size("col")
    seqs, own, channels = alignment.shape
    total = pair_cotangent.shape[1]
    depth = Z // count
    mask = sequence_mask.T
    turn = [(0, 1), (1, 0)]
    mate = lax.ppermute(mask, "row", turn)
    fetched = [alignment, norm_mean.T, norm_inverse.T, input_bias[None, :], residue_mask[None, :]]
    passed = [mask, norm_gain[None, :], norm_shift[None, :], input_weight.T, pair_cotangent, output_weight]
    operands = [pltpu.with_memory_space_constraint(a, pltpu.HBM) for a in fetched + passed]
    mask, gain, shift, weight, cotangent, out_weight, hat, stats, present, *messages = call(
        prepare,
        [shape(a.shape, a.dtype) for a in passed]
        + [shape((own, seqs, channels), F32), shape((LANES, LANES), F32), shape((own, LANES), F32)]
        + [shape((MESSAGE, LANES), BF16)] * count,
        [HBM_SPEC] * len(operands),
        operands,
        [pltpu.VMEM(a.shape, a.dtype) for a in fetched]
        + [
            pltpu.VMEM((2, seqs * own, LANES), F32),
            pltpu.VMEM((PROJ_ROWS, LANES), F32),
            pltpu.VMEM((own * total, Z), F32),
            pltpu.VMEM((own // 2, Z, LANES), BF16),
            pltpu.VMEM((LANES, LANES), F32),
            pltpu.SemaphoreType.DMA((len(operands) - 1,)),
            pltpu.SemaphoreType.DMA,
        ],
    )
    messages = call(
        add_masks,
        [shape((MESSAGE, LANES), BF16)] * count,
        [VMEM_SPEC] * (3 + count),
        [mask, present, mate, *messages],
        aliases={3 + k: k for k in range(count)},
    )
    messages = [messages[0]] + [
        lax.ppermute(messages[k], "col", [(c, c ^ ORDER[k]) for c in range(count)]) for k in range(1, count)
    ]
    (cots,) = call(
        collect,
        [shape((count, MESSAGE - COT_AT, LANES), BF16)],
        [VMEM_SPEC] * count,
        messages,
    )
    mate_cots = lax.ppermute(cots, "row", turn)
    every, gathered, scale_own, scale_twice, live, left_grad = call(
        left_part,
        [
            shape((P_SIZE * total, LANES), F32),
            shape((P_SIZE * total, LANES), BF16),
            shape((total, LANES), F32),
            shape((total, LANES), F32),
            shape((own, LANES), F32),
            shape((own * P_SIZE, LANES), F32),
        ],
        [VMEM_SPEC] * (2 + count),
        [cotangent, out_weight, *messages],
        [
            pltpu.VMEM((total, LANES), F32),
            pltpu.VMEM((total, LANES), F32),
            pltpu.VMEM((own * total, Z), BF16),
            pltpu.VMEM((own * P_SIZE, P_SIZE * total), BF16),
            pltpu.VMEM((P_SIZE * P_SIZE, LANES), F32),
        ],
    )
    normed_grads, keep = call(
        sums_part,
        [shape((own, seqs, channels), F32), shape((PARTIAL, LANES), F32)],
        [VMEM_SPEC] * 13,
        [cots, mate_cots, out_weight, every, gathered, scale_own, scale_twice, live, left_grad, hat, gain, shift, weight],
        [
            pltpu.VMEM((own * total, Z), F32),
            pltpu.VMEM((own * total, Z), BF16),
            pltpu.VMEM((count * own // 4 * depth, 2 * LANES), BF16),
            pltpu.VMEM((own * P_SIZE, P_SIZE * total), BF16),
            pltpu.VMEM((4, 4 * total, 2 * LANES), BF16),
            pltpu.VMEM((count * own // 4, P_SIZE * depth, 4 * seqs), BF16),
            pltpu.VMEM((LANES, LANES), F32),
        ],
    )
    given = lax.ppermute(keep, "row", turn)
    (activation,) = call(
        activations,
        [shape(alignment.shape, BF16)],
        [VMEM_SPEC] * 4,
        [normed_grads, hat, stats, gain],
        [pltpu.VMEM((2, seqs * own, LANES), F32)],
    )
    (partial,) = call(pack, [shape((SENT, LANES), BF16)], [VMEM_SPEC] * 2, [keep, given])
    parts = []
    for pair in zip(*PEERS):
        turns = [
            (row * count + c, row * count + (c ^ pair[row])) for row in range(2) if pair[row] for c in range(count)
        ]
        parts.append(lax.ppermute(partial, ("row", "col"), turns))
    (received,) = call(
        stack, [shape((len(parts), SENT, LANES), BF16)], [VMEM_SPEC] * len(parts), parts
    )
    theirs = lax.ppermute(received, "row", turn)
    input_grad, bias_grad, weight_grad, out_bias_grad, gain_grad, shift_grad = call(
        finish,
        [
            shape((2 * P_SIZE, channels), F32),
            shape((1, 2 * P_SIZE), F32),
            shape((P_SIZE * P_SIZE, Z), F32),
            shape((1, Z), F32),
            shape((1, channels), F32),
            shape((1, channels), F32),
        ],
        [VMEM_SPEC] * 3,
        [partial, received, theirs],
        [pltpu.VMEM((count, SENT, LANES), BF16)],
    )
    return (activation, input_grad.T, bias_grad[0], weight_grad, out_bias_grad[0], gain_grad[0], shift_grad[0])


def local(*args):
    alignment, cotangent = args[0], args[8]
    seqs, own, channels = alignment.shape
    total = cotangent.shape[1]
    count = lax.axis_size("col")
    fits = (
        2 * seqs == LANES
        and 2 * total == LANES
        and own == 8
        and channels == 2 * LANES
        and count == 8
        and lax.axis_size("row") == 2
    )
    return tiled(*args) if fits else general(*args)


def solution(mesh):
    in_specs = (
        P(("group", "row"), "col", None),
        P(("group", "row"), "col"),
        P(("group", "row"), "col"),
        P(),
        P(),
        P(),
        P(),
        P(),
        P("col", "group", None),
        P("group"),
        P(("group", "row"), "col"),
    )
    out_specs = (
        P(("group", "row"), "col", None),
        P("group", None),
        P("group"),
        P("group", None),
        P("group"),
        P("group"),
        P("group"),
    )
    return jax.shard_map(local, mesh=mesh, in_specs=in_specs, out_specs=out_specs, check_vma=False)
```

```python
import math

import jax
import jax.numpy as jnp
from jax import lax
from jax.experimental import pallas as pl
from jax.experimental.pallas import tpu as pltpu
from jax.sharding import PartitionSpec as P

C = 256
P_SIZE = 32
Z = 128


def normalize(alignment, norm_mean, norm_inverse, norm_gain, norm_shift):
    hatted = (alignment.astype(jnp.float32) - norm_mean[..., None]) * norm_inverse[..., None]
    normed = (hatted * norm_gain + norm_shift).astype(jnp.bfloat16)
    return (hatted, normed)


def project(normed, input_weight, input_bias, live):
    flat = normed.reshape(-1, normed.shape[-1])
    projected = jnp.dot(flat, input_weight, preferred_element_type=jnp.float32) + input_bias
    projected = projected.reshape(normed.shape[:-1] + (input_weight.shape[1],)) * live[..., None]
    return projected.astype(jnp.bfloat16)


def contract(left, right, counts, cotangent, pair_live, output_weight):
    sequence_count, row_count, _ = left.shape
    column_total = right.shape[1]
    width = math.gcd(column_total, 128)
    left_acc = jnp.zeros(left.shape, jnp.float32)
    weight_acc = jnp.zeros((P_SIZE * P_SIZE, Z), jnp.float32)
    bias_acc = jnp.zeros((Z,), jnp.float32)
    pieces = []
    for offset in range(0, column_total, width):
        right_cols = right[:, offset : offset + width]
        scale = pair_live[:, offset : offset + width] / jnp.maximum(
            counts[:, offset : offset + width], 1.0
        )
        pair_grad = cotangent[:, offset : offset + width].astype(jnp.float32) * scale[..., None]
        pair_low = pair_grad.astype(jnp.bfloat16).reshape(-1, Z)
        outer_grad = jnp.einsum(
            "ne,ke->nk", pair_low, output_weight, preferred_element_type=jnp.float32
        )
        outer_grad = outer_grad.astype(jnp.bfloat16).reshape(row_count, width, P_SIZE, P_SIZE)
        left_acc = left_acc + jnp.einsum(
            "ijpq,sjq->sip", outer_grad, right_cols, preferred_element_type=jnp.float32
        )
        pieces.append(
            jnp.einsum("ijpq,sip->sjq", outer_grad, left, preferred_element_type=jnp.float32)
        )
        outer = jnp.einsum(
            "sip,sjq->ijpq", left, right_cols, preferred_element_type=jnp.float32
        ).reshape(-1, P_SIZE * P_SIZE)
        outer_high = outer.astype(jnp.bfloat16)
        outer_rest = (outer - outer_high.astype(jnp.float32)).astype(jnp.bfloat16)
        weight_acc = weight_acc + jnp.einsum(
            "nk,ne->ke", outer_high, pair_low, preferred_element_type=jnp.float32
        )
        weight_acc = weight_acc + jnp.einsum(
            "nk,ne->ke", outer_rest, pair_low, preferred_element_type=jnp.float32
        )
        bias_acc = bias_acc + jnp.sum(pair_grad, axis=(0, 1))
    right_out = jnp.concatenate(pieces, axis=1)
    return (left_acc, right_out, weight_acc, bias_acc)


def general(
    alignment,
    norm_mean,
    norm_inverse,
    norm_gain,
    norm_shift,
    input_weight,
    input_bias,
    output_weight,
    pair_cotangent,
    residue_mask,
    sequence_mask,
):
    sequence_count, residue_count = sequence_mask.shape
    residue_total = residue_mask.shape[0]
    column = lax.axis_index("col")
    residue_float = residue_mask.astype(jnp.float32)
    own_residues = lax.dynamic_slice_in_dim(residue_float, column * residue_count, residue_count, 0)
    own_mask = lax.dynamic_slice_in_dim(residue_mask, column * residue_count, residue_count, 0)
    live_int = sequence_mask * own_mask[None, :]
    live = live_int.astype(jnp.float32)
    hatted, normed = normalize(alignment, norm_mean, norm_inverse, norm_gain, norm_shift)
    projected = project(normed, input_weight, input_bias, live)
    left = projected[..., :P_SIZE]
    right = projected[..., P_SIZE:]
    gathered, mask_cols = (
        lax.all_gather(
            right.reshape(sequence_count, residue_count * P_SIZE), "col", axis=1, tiled=True
        ),
        lax.all_gather(live_int, "col", axis=1, tiled=True),
    )
    right_all = gathered.reshape(sequence_count, residue_total, P_SIZE)
    partial_counts = jnp.dot(live.T, mask_cols.astype(jnp.float32), precision=lax.Precision.HIGHEST)
    counts = lax.psum(partial_counts, "row")
    pair_live = own_residues[:, None] * residue_float[None, :]
    left_grad, right_part, weight_out, bias_out = contract(
        left, right_all, counts, pair_cotangent, pair_live, output_weight
    )
    bias_out = bias_out / lax.axis_size("row")
    summed = lax.psum_scatter(
        right_part.reshape(sequence_count, residue_total * P_SIZE),
        "col",
        scatter_dimension=1,
        tiled=True,
    )
    right_grad = summed.reshape(sequence_count, residue_count, P_SIZE)
    proj_grad = jnp.concatenate([left_grad, right_grad], axis=-1) * live[..., None]
    proj_low = proj_grad.astype(jnp.bfloat16).reshape(-1, 2 * P_SIZE)
    flat_normed = normed.reshape(-1, C)
    weight_part = jnp.einsum("nc,nk->ck", flat_normed, proj_low, preferred_element_type=jnp.float32)
    bias_part = jnp.sum(proj_grad, axis=(0, 1))
    normed_grad = jnp.einsum(
        "nk,ck->nc", proj_low, input_weight, preferred_element_type=jnp.float32
    ).reshape(hatted.shape)
    gain_part = jnp.sum(normed_grad * hatted, axis=(0, 1))
    shift_part = jnp.sum(normed_grad, axis=(0, 1))
    hat_grad = normed_grad * norm_gain
    centered = (
        hat_grad
        - jnp.mean(hat_grad, axis=-1, keepdims=True)
        - hatted * jnp.mean(hat_grad * hatted, axis=-1, keepdims=True)
    )
    activation_grad = (norm_inverse[..., None] * centered).astype(jnp.bfloat16)
    totals = lax.psum(
        (weight_part, bias_part, gain_part, shift_part, weight_out, bias_out), ("row", "col")
    )
    return (activation_grad, totals[0], totals[1], totals[4], totals[5], totals[2], totals[3])


LANES = 128
PROJ_ROWS = 256
COT_AT = 256
MESSAGE = 320
DEAD = 32768.0
SMALL_AT = 256
PARTIAL = 264
SENT = 272
PEERS = ((0, 6, 1, 5), (2, 4, 3, 7))
ORDER = (0, 6, 1, 7, 2, 5, 3, 4)
VMEM = pltpu.CompilerParams(vmem_limit_bytes=24 * 1024 * 1024)
F32 = jnp.float32
BF16 = jnp.bfloat16


def dot_nt(a, b):
    return lax.dot_general(a, b, (((1,), (1,)), ((), ())), preferred_element_type=F32)


def dot_nn(a, b):
    return lax.dot_general(a, b, (((1,), (0,)), ((), ())), preferred_element_type=F32)


def low_lanes(shape):
    return lax.broadcasted_iota(jnp.int32, shape, 1) < LANES // 2


def swap_halves(x):
    return pltpu.roll(x, LANES // 2, 1)


def strided(wide, start, size, stride):
    return jnp.concatenate([wide[h, pl.ds(start, size, stride=stride), :] for h in range(2)], axis=1)


def prepare(*rest):
    sources = rest[:11]
    gain, shift, weight, cotangent, out_weight, hat, stats, present = rest[11:19]
    messages = rest[19:-13]
    count = len(messages)
    alignment, mean, inverse, bias, residue, mask, wide, packed, cot, turned, square, arrived, late = rest[-13:]
    targets = (alignment, mean, inverse, bias, residue, mask, gain, shift, weight)
    first = pltpu.make_async_copy(sources[-2], cotangent, late.at[0])
    first.start()
    copies = [pltpu.make_async_copy(f, t, arrived.at[i]) for i, (f, t) in enumerate(zip(sources, targets))]
    for copy in copies:
        copy.start()
    last = pltpu.make_async_copy(sources[-1], out_weight, late.at[1])
    last.start()
    col, row = lax.axis_index("col"), lax.axis_index("row")
    seqs, own, channels = alignment.shape
    total = cotangent.shape[1]
    depth = Z // count
    first.wait()

    @pl.when(row == 0)
    def _():
        cot[...] = cotangent[...].astype(F32).reshape(own * total, Z)
        for k, message in enumerate(messages):
            peer = col ^ ORDER[k]
            message[COT_AT:MESSAGE, :] = jnp.concatenate(
                [cot[pl.ds(own * peer + j, own, stride=total), :] for j in range(own)], axis=0
            ).astype(BF16)

    @pl.when(row != 0)
    def _():
        for i in range(own // 2):
            pair = jnp.concatenate([cotangent[i], cotangent[i + own // 2]], axis=0).astype(F32)
            turned[i] = pair.T.astype(BF16)
        for k, message in enumerate(messages):
            at = pl.multiple_of((col ^ ORDER[k]) * depth, depth)
            for i in range(own // 2):
                message[COT_AT + i * depth : COT_AT + (i + 1) * depth, :] = turned[i, pl.ds(at, depth), :]

    for copy in copies:
        copy.wait()
    square[0:own, :seqs] = mean[...]
    square[own : 2 * own, :seqs] = inverse[...]
    square[2 * own : 3 * own, : 2 * P_SIZE] = jnp.broadcast_to(bias[...], (own, 2 * P_SIZE))
    square[3 * own : 4 * own, :total] = jnp.broadcast_to(residue[...].astype(F32), (own, total))
    stats[...] = square[...].T
    present[...] = jnp.broadcast_to(stats[:total, 3 * own : 3 * own + 1], (total, LANES))
    live = mask[...].astype(F32) * present[pl.ds(pl.multiple_of(col * own, own), own), :seqs]
    values = alignment[...].astype(F32)
    for h in range(2):
        wide[h] = values[:, :, h * LANES : (h + 1) * LANES].reshape(seqs * own, LANES)
    for r in range(own):
        hatted = (strided(wide, r, seqs, own) - stats[:seqs, r : r + 1]) * stats[
            :seqs, own + r : own + r + 1
        ]
        hat[r] = hatted
        normed = (hatted * gain[...] + shift[...]).astype(BF16)
        projected = dot_nt(weight[...], normed) + stats[: 2 * P_SIZE, 2 * own : 2 * own + 1]
        projected = jnp.where(live[r : r + 1] > 0.0, projected, DEAD)
        packed[pl.ds(r, P_SIZE, stride=own), :] = jnp.concatenate(
            [projected[:P_SIZE], projected[P_SIZE:]], axis=1
        )
    shared = packed[...].astype(BF16)
    for message in messages:
        message[0:PROJ_ROWS, :] = shared
    last.wait()


def collect(*rest):
    messages, out = rest[:-2], rest[-2]
    live = rest[-1]
    col = lax.axis_index("col")
    count = len(messages)
    own = live.shape[0] // count
    for k, message in enumerate(messages):
        peer = col ^ ORDER[k]
        out[peer] = message[COT_AT:MESSAGE, :]
        here = message[0 : 2 * own, :].astype(F32)[:own]
        live[pl.ds(pl.multiple_of(peer * own, own), own), :] = jnp.where(here < 0.5 * DEAD, 1.0, 0.0)
    out[count] = live[...].astype(BF16)


def interleave(product, target, group, at):
    half = LANES // 2
    low = low_lanes((P_SIZE, LANES))
    for a in range(0, product.shape[0] // P_SIZE, 2):
        for b in range(0, group, 2):
            first = product[a * P_SIZE : (a + 1) * P_SIZE, b * half : (b + 2) * half]
            second = product[(a + 1) * P_SIZE : (a + 2) * P_SIZE, b * half : (b + 2) * half]
            lanes = slice((at + a) * half, (at + a + 2) * half)
            target[b * P_SIZE : (b + 1) * P_SIZE, lanes] = jnp.where(
                low, first, swap_halves(second)
            ).astype(BF16)
            target[(b + 1) * P_SIZE : (b + 2) * P_SIZE, lanes] = jnp.where(
                low, swap_halves(first), second
            ).astype(BF16)


BLOCK = 8
STEPS = 3


def arrange(out_weight, *rest):
    messages = rest[:-4]
    every, gathered, by_second, wide = rest[-4:]
    col = lax.axis_index("col")
    own = PROJ_ROWS // P_SIZE
    total = own * len(messages)
    wide[...] = out_weight[...].astype(F32)
    for k, message in enumerate(messages):
        at = pl.multiple_of((col ^ ORDER[k]) * own, own)
        block = message[0:PROJ_ROWS, :].astype(F32)
        block = jnp.where(block < 0.5 * DEAD, block, 0.0)
        for q in range(P_SIZE):
            every[pl.ds(q * total + at, own), :] = block[q * own : (q + 1) * own]
    for q in range(P_SIZE):
        by_second[q * P_SIZE : (q + 1) * P_SIZE, :] = wide[pl.ds(q, P_SIZE, stride=P_SIZE), :].astype(BF16)
    gathered[...] = every[...].astype(BF16)


def quad_members(quad):
    base = quad // 2 * 8 + quad % 2 * 2
    return ((base, base + 4), (base + 1, base + 5))


def take_turns(*tracks):
    results = [None] * len(tracks)
    going = set(range(len(tracks)))
    while going:
        for t, (track, steps) in enumerate(tracks):
            for _ in range(steps):
                if t in going:
                    try:
                        next(track)
                    except StopIteration as end:
                        results[t] = end.value
                        going.discard(t)
    return results


def sums_part(
    pieces, mate, cotangent, by_second, present, out_weight, every, gathered, hat, gain, shift, weight, normed_grads, keep, turned, grad_own, grad_turned, grad_slice, outer, scales, corner, mixed, square
):
    col, row = lax.axis_index("col"), lax.axis_index("row")
    count = pieces.shape[0] - 1
    own, seqs, channels = hat.shape
    total = grad_turned.shape[0] // own
    depth = Z // count
    half = LANES // 2
    pairs = own // 2
    mine = row == 0
    here = present[...].astype(BF16)
    counts = sum(
        dot_nt(m, jnp.concatenate([m, m], axis=0)) for m in (pieces[count], mate[count])
    )
    scales[...] = (
        dot_nt(here, jnp.concatenate([here, here], axis=0))
        * (1.0 / LANES)
        / jnp.maximum(counts * 0.5, 1.0)
    )
    own_at = pl.ds(pl.multiple_of(col * own, own), own)
    scale_own = dot_nt(here, present[own_at, :].astype(BF16)) * (1.0 / LANES)
    counts_own = jnp.zeros((total, own), F32)
    for m in (pieces, mate):
        square[0:total, :] = m[count].astype(F32)
        counts_own = counts_own + dot_nt(m[count], square[own_at, :].astype(BF16))
    scale_own = scale_own / jnp.maximum(counts_own * 0.5, 1.0)
    square[0:total, :] = pieces[count].astype(F32)
    live = square[own_at, :]
    low = low_lanes((own, LANES))
    bias_acc = jnp.zeros((depth, LANES), F32)
    for c in range(count):
        one, two = pieces[c].astype(F32), mate[c].astype(F32)
        block = jnp.where(mine, one, two)
        for j in range(own):
            turned[j * total + c * own : j * total + (c + 1) * own, :] = block[j * own : (j + 1) * own]
        block = jnp.where(mine, two, one)
        tile = scales[c * own : (c + 1) * own, :]
        tile = jnp.where(low, tile, jnp.concatenate([tile[pairs:], tile[:pairs]], axis=0))
        for i in range(pairs):
            piece = block[i * depth : (i + 1) * depth] * tile[i : i + 1, :]
            bias_acc = bias_acc + piece
            grad_slice[
                (c * 2 + i // 2) * depth : (c * 2 + i // 2 + 1) * depth,
                i % 2 * LANES : (i % 2 + 1) * LANES,
            ] = piece.astype(BF16)
    for i in range(own):
        rows = slice(i * total, (i + 1) * total)
        grad_own[rows, :] = (cotangent[i].astype(F32) * scale_own[:, i : i + 1]).astype(BF16)
        grad_turned[rows, :] = (turned[rows, :] * scale_own[:, i : i + 1]).astype(BF16)

    def grads():
        for a in range(0, P_SIZE, BLOCK):
            rows = slice(a * P_SIZE, (a + BLOCK) * P_SIZE)
            interleave(dot_nt(by_second[rows, :], grad_own[...]), outer.at[0], own, a)
            yield
        left_grad = swap_halves(dot_nn(outer[0], gathered[...]))
        yield
        for a in range(0, P_SIZE, BLOCK):
            rows = slice(a * P_SIZE, (a + BLOCK) * P_SIZE)
            interleave(dot_nt(out_weight[rows, :], grad_turned[...]), outer.at[1], own, a)
            yield
        right_grad = dot_nn(outer[1], gathered[...])
        yield
        input_acc = jnp.zeros((2 * P_SIZE, channels), F32)
        proj_acc = jnp.zeros((2 * P_SIZE, seqs), F32)
        gain_acc = jnp.zeros((1, channels), F32)
        shift_acc = jnp.zeros((1, channels), F32)
        for r in range(own):
            hatted = hat[r]
            normed = (hatted * gain[...] + shift[...]).astype(BF16)
            spot = slice(r * P_SIZE, (r + 1) * P_SIZE)
            proj_grad = jnp.concatenate([left_grad[spot, :seqs], right_grad[spot, :seqs]], axis=0)
            proj_grad = proj_grad * live[r : r + 1, :seqs]
            proj_acc = proj_acc + proj_grad
            input_acc = input_acc + dot_nn(proj_grad.astype(BF16), normed)
            normed_grad = dot_nn(proj_grad.T.astype(BF16), weight[...])
            gain_acc = gain_acc + jnp.sum(normed_grad * hatted, axis=0, keepdims=True)
            shift_acc = shift_acc + jnp.sum(normed_grad, axis=0, keepdims=True)
            normed_grads[r] = normed_grad
            yield
        return (input_acc, proj_acc, gain_acc, shift_acc)

    quads = count * own // 4

    def slices():
        low = low_lanes((total, LANES))
        corner[...] = jnp.zeros_like(corner)
        for q in range(P_SIZE):
            block = every[q * total : (q + 1) * total, :]
            here = jnp.where(low, 0.0, block)
            moved = swap_halves(here).astype(BF16)
            here = here.astype(BF16)
            slot = q % corner.shape[0]
            for at in range(4):
                lanes = slice(at // 2 * LANES, (at // 2 + 1) * LANES)
                corner[slot, at * total : (at + 1) * total, lanes] = here if at % 2 else moved
            mixed[:, q * depth : (q + 1) * depth, :] = (
                dot_nn(grad_slice[...], corner[slot]).astype(BF16).reshape(quads, depth, 4 * total)
            )
            yield
        low = low_lanes((P_SIZE, LANES))
        weight_acc = jnp.zeros((P_SIZE * depth, P_SIZE), F32)
        for quad in range(quads):
            rhs = []
            for pair in quad_members(quad):
                one, two = (every[pl.ds(i, P_SIZE, stride=total), :] for i in pair)
                rhs.append(jnp.where(low, one, swap_halves(two)))
            weight_acc = weight_acc + dot_nt(mixed[quad], jnp.concatenate(rhs, axis=1).astype(BF16))
            yield
        return weight_acc

    (input_acc, proj_acc, gain_acc, shift_acc), weight_acc = take_turns((grads(), 1), (slices(), STEPS))
    group = P_SIZE * depth // 4
    weight_acc = jnp.concatenate([weight_acc[b * group : (b + 1) * group] for b in range(4)], axis=1)

    square[...] = jnp.zeros((LANES, LANES), F32)
    square[0 : 2 * P_SIZE, :seqs] = proj_acc
    square[half : half + depth, :] = bias_acc * 0.5
    sums = jnp.sum(square[...].T, axis=0, keepdims=True)
    keep[0:LANES, :] = weight_acc
    for h in range(2):
        lanes = slice(h * LANES, (h + 1) * LANES)
        keep[LANES + h * half : LANES + (h + 1) * half, :] = input_acc[:, lanes]
        keep[SMALL_AT + h : SMALL_AT + h + 1, :] = gain_acc[:, lanes]
        keep[SMALL_AT + 2 + h : SMALL_AT + 3 + h, :] = shift_acc[:, lanes]
    keep[SMALL_AT + 4 : PARTIAL, :] = jnp.concatenate([sums, jnp.zeros((3, LANES), F32)], axis=0)


def activations(normed_grads, hat, stats, gain, activation, wide):
    own, seqs, channels = hat.shape
    for r in range(own):
        hatted = hat[r]
        hat_grad = normed_grads[r] * gain[...]
        first = jnp.sum(hat_grad, axis=1, keepdims=True) * (1.0 / channels)
        second = jnp.sum(hat_grad * hatted, axis=1, keepdims=True) * (1.0 / channels)
        result = stats[:seqs, own + r : own + r + 1] * (hat_grad - first - hatted * second)
        for h in range(2):
            wide[h, pl.ds(r, seqs, stride=own), :] = result[:, h * LANES : (h + 1) * LANES]
    activation[...] = jnp.concatenate(
        [wide[h].reshape(seqs, own, LANES) for h in range(2)], axis=2
    ).astype(BF16)


def pack(kept, given, partial):
    both = kept[...] + given[...]
    high = both.astype(BF16)
    small = both[SMALL_AT:] - high[SMALL_AT:].astype(F32)
    partial[...] = jnp.concatenate([high, small.astype(BF16)], axis=0)


def stack(*rest):
    for k, part in enumerate(rest[:-1]):
        rest[-1][k] = part[...]


def finish(own, received, mate, input_out, bias_out, weight_out, out_bias_out, gain_out, shift_out, ordered):
    col, row = lax.axis_index("col"), lax.axis_index("row")
    count = ordered.shape[0]
    depth = Z // count
    half = LANES // 2
    lane = lax.broadcasted_iota(jnp.int32, (1, LANES), 1)
    ordered[col] = own[...]
    for k, (one, two) in enumerate(zip(*PEERS)):
        ordered[col ^ jnp.where(row == 0, one, two)] = received[k]
        ordered[col ^ jnp.where(row == 0, two, one)] = mate[k]
    ordered[col] = own[...]
    for a in range(8):
        turned = jnp.concatenate(
            [ordered[c, a * depth : (a + 1) * depth] for c in range(count)], axis=0
        ).astype(F32).T
        for b in range(4):
            weight_out[pl.ds(8 * b + a, P_SIZE, stride=P_SIZE), :] = turned[b * P_SIZE : (b + 1) * P_SIZE]
    input_acc = jnp.zeros((LANES, LANES), F32)
    small_acc = jnp.zeros((8, LANES), F32)
    out_bias = jnp.zeros((1, LANES), F32)
    for c in range(count):
        input_acc = input_acc + ordered[c, LANES:SMALL_AT].astype(F32)
        both = ordered[c, SMALL_AT:].astype(F32)
        small = both[:8] + both[8:]
        small_acc = small_acc + small
        bias = pltpu.roll(small[4:5], (c * depth + half) % LANES, 1)
        out_bias = jnp.where((lane >= c * depth) & (lane < (c + 1) * depth), bias, out_bias)
    for h in range(2):
        lanes = slice(h * LANES, (h + 1) * LANES)
        input_out[:, lanes] = input_acc[h * half : (h + 1) * half]
        gain_out[:, lanes] = small_acc[h : h + 1]
        shift_out[:, lanes] = small_acc[2 + h : 3 + h]
    bias_out[...] = small_acc[4:5, :half]
    out_bias_out[...] = out_bias


def shape(dims, dtype):
    return jax.ShapeDtypeStruct(dims, dtype)


VMEM_SPEC = pl.BlockSpec(memory_space=pltpu.VMEM)
HBM_SPEC = pl.BlockSpec(memory_space=pltpu.HBM)


def call(kernel, outputs, specs, arguments, scratch=(), aliases=None):
    return pl.pallas_call(
        kernel,
        out_shape=outputs,
        in_specs=specs,
        out_specs=[VMEM_SPEC] * len(outputs),
        scratch_shapes=list(scratch),
        input_output_aliases=aliases or {},
        compiler_params=VMEM,
        name=kernel.__name__,
    )(*arguments)


def tiled(
    alignment,
    norm_mean,
    norm_inverse,
    norm_gain,
    norm_shift,
    input_weight,
    input_bias,
    output_weight,
    pair_cotangent,
    residue_mask,
    sequence_mask,
):
    count = lax.axis_size("col")
    seqs, own, channels = alignment.shape
    total = pair_cotangent.shape[1]
    depth = Z // count
    turn = [(0, 1), (1, 0)]
    fetched = [alignment, norm_mean.T, norm_inverse.T, input_bias[None, :], residue_mask[None, :], sequence_mask.T]
    passed = [norm_gain[None, :], norm_shift[None, :], input_weight.T, pair_cotangent, output_weight]
    operands = [pltpu.with_memory_space_constraint(a, pltpu.HBM) for a in fetched + passed]
    gain, shift, weight, cotangent, out_weight, hat, stats, present, *messages = call(
        prepare,
        [shape(a.shape, a.dtype) for a in passed]
        + [shape((own, seqs, channels), F32), shape((LANES, LANES), F32), shape((total, LANES), F32)]
        + [shape((MESSAGE, LANES), BF16)] * count,
        [HBM_SPEC] * len(operands),
        operands,
        [pltpu.VMEM(a.shape, a.dtype) for a in fetched]
        + [
            pltpu.VMEM((2, seqs * own, LANES), F32),
            pltpu.VMEM((PROJ_ROWS, LANES), F32),
            pltpu.VMEM((own * total, Z), F32),
            pltpu.VMEM((own // 2, Z, LANES), BF16),
            pltpu.VMEM((LANES, LANES), F32),
            pltpu.SemaphoreType.DMA((len(operands) - 2,)),
            pltpu.SemaphoreType.DMA((2,)),
        ],
    )
    messages = [messages[0]] + [
        lax.ppermute(messages[k], "col", [(c, c ^ ORDER[k]) for c in range(count)]) for k in range(1, count)
    ]
    (pieces,) = call(
        collect,
        [shape((count + 1, total, LANES), BF16)],
        [VMEM_SPEC] * count,
        messages,
        [pltpu.VMEM((total, LANES), F32)],
    )
    mate_pieces = lax.ppermute(pieces, "row", turn)
    every, gathered, by_second = call(
        arrange,
        [
            shape((P_SIZE * total, LANES), F32),
            shape((P_SIZE * total, LANES), BF16),
            shape((P_SIZE * P_SIZE, LANES), BF16),
        ],
        [VMEM_SPEC] * (1 + count),
        [out_weight, *messages],
        [pltpu.VMEM((P_SIZE * P_SIZE, LANES), F32)],
    )
    normed_grads, keep = call(
        sums_part,
        [shape((own, seqs, channels), F32), shape((PARTIAL, LANES), F32)],
        [VMEM_SPEC] * 12,
        [pieces, mate_pieces, cotangent, by_second, present, out_weight, every, gathered, hat, gain, shift, weight],
        [
            pltpu.VMEM((own * total, Z), F32),
            pltpu.VMEM((own * total, Z), BF16),
            pltpu.VMEM((own * total, Z), BF16),
            pltpu.VMEM((count * own // 4 * depth, 2 * LANES), BF16),
            pltpu.VMEM((2, own * P_SIZE, P_SIZE * total), BF16),
            pltpu.VMEM((total, LANES), F32),
            pltpu.VMEM((4, 4 * total, 2 * LANES), BF16),
            pltpu.VMEM((count * own // 4, P_SIZE * depth, 4 * seqs), BF16),
            pltpu.VMEM((LANES, LANES), F32),
        ],
    )
    given = lax.ppermute(keep, "row", turn)
    (activation,) = call(
        activations,
        [shape(alignment.shape, BF16)],
        [VMEM_SPEC] * 4,
        [normed_grads, hat, stats, gain],
        [pltpu.VMEM((2, seqs * own, LANES), F32)],
    )
    (partial,) = call(
        pack, [shape((SENT, LANES), BF16)], [VMEM_SPEC] * 2, [keep, given]
    )
    parts = []
    for pair in zip(*PEERS):
        turns = [
            (row * count + c, row * count + (c ^ pair[row])) for row in range(2) if pair[row] for c in range(count)
        ]
        parts.append(lax.ppermute(partial, ("row", "col"), turns))
    (received,) = call(
        stack, [shape((len(parts), SENT, LANES), BF16)], [VMEM_SPEC] * len(parts), parts
    )
    theirs = lax.ppermute(received, "row", turn)
    input_grad, bias_grad, weight_grad, out_bias_grad, gain_grad, shift_grad = call(
        finish,
        [
            shape((2 * P_SIZE, channels), F32),
            shape((1, 2 * P_SIZE), F32),
            shape((P_SIZE * P_SIZE, Z), F32),
            shape((1, Z), F32),
            shape((1, channels), F32),
            shape((1, channels), F32),
        ],
        [VMEM_SPEC] * 3,
        [partial, received, theirs],
        [pltpu.VMEM((count, SENT, LANES), BF16)],
    )
    return (activation, input_grad.T, bias_grad[0], weight_grad, out_bias_grad[0], gain_grad[0], shift_grad[0])


def local(*args):
    alignment, cotangent = args[0], args[8]
    seqs, own, channels = alignment.shape
    total = cotangent.shape[1]
    count = lax.axis_size("col")
    fits = (
        2 * seqs == LANES
        and 2 * total == LANES
        and own == 8
        and channels == 2 * LANES
        and count == 8
        and lax.axis_size("row") == 2
    )
    return tiled(*args) if fits else general(*args)


def solution(mesh):
    in_specs = (
        P(("group", "row"), "col", None),
        P(("group", "row"), "col"),
        P(("group", "row"), "col"),
        P(),
        P(),
        P(),
        P(),
        P(),
        P("col", "group", None),
        P("group"),
        P(("group", "row"), "col"),
    )
    out_specs = (
        P(("group", "row"), "col", None),
        P("group", None),
        P("group"),
        P("group", None),
        P("group"),
        P("group"),
        P("group"),
    )
    return jax.shard_map(local, mesh=mesh, in_specs=in_specs, out_specs=out_specs, check_vma=False)
```

```python
import math

import jax
import jax.numpy as jnp
from jax import lax
from jax.experimental import pallas as pl
from jax.experimental.pallas import tpu as pltpu
from jax.sharding import PartitionSpec as P

C = 256
P_SIZE = 32
Z = 128


def normalize(alignment, norm_mean, norm_inverse, norm_gain, norm_shift):
    hatted = (alignment.astype(jnp.float32) - norm_mean[..., None]) * norm_inverse[..., None]
    normed = (hatted * norm_gain + norm_shift).astype(jnp.bfloat16)
    return (hatted, normed)


def project(normed, input_weight, input_bias, live):
    flat = normed.reshape(-1, normed.shape[-1])
    projected = jnp.dot(flat, input_weight, preferred_element_type=jnp.float32) + input_bias
    projected = projected.reshape(normed.shape[:-1] + (input_weight.shape[1],)) * live[..., None]
    return projected.astype(jnp.bfloat16)


def contract(left, right, counts, cotangent, pair_live, output_weight):
    sequence_count, row_count, _ = left.shape
    column_total = right.shape[1]
    width = math.gcd(column_total, 128)
    left_acc = jnp.zeros(left.shape, jnp.float32)
    weight_acc = jnp.zeros((P_SIZE * P_SIZE, Z), jnp.float32)
    bias_acc = jnp.zeros((Z,), jnp.float32)
    pieces = []
    for offset in range(0, column_total, width):
        right_cols = right[:, offset : offset + width]
        scale = pair_live[:, offset : offset + width] / jnp.maximum(
            counts[:, offset : offset + width], 1.0
        )
        pair_grad = cotangent[:, offset : offset + width].astype(jnp.float32) * scale[..., None]
        pair_low = pair_grad.astype(jnp.bfloat16).reshape(-1, Z)
        outer_grad = jnp.einsum(
            "ne,ke->nk", pair_low, output_weight, preferred_element_type=jnp.float32
        )
        outer_grad = outer_grad.astype(jnp.bfloat16).reshape(row_count, width, P_SIZE, P_SIZE)
        left_acc = left_acc + jnp.einsum(
            "ijpq,sjq->sip", outer_grad, right_cols, preferred_element_type=jnp.float32
        )
        pieces.append(
            jnp.einsum("ijpq,sip->sjq", outer_grad, left, preferred_element_type=jnp.float32)
        )
        outer = jnp.einsum(
            "sip,sjq->ijpq", left, right_cols, preferred_element_type=jnp.float32
        ).reshape(-1, P_SIZE * P_SIZE)
        outer_high = outer.astype(jnp.bfloat16)
        outer_rest = (outer - outer_high.astype(jnp.float32)).astype(jnp.bfloat16)
        weight_acc = weight_acc + jnp.einsum(
            "nk,ne->ke", outer_high, pair_low, preferred_element_type=jnp.float32
        )
        weight_acc = weight_acc + jnp.einsum(
            "nk,ne->ke", outer_rest, pair_low, preferred_element_type=jnp.float32
        )
        bias_acc = bias_acc + jnp.sum(pair_grad, axis=(0, 1))
    right_out = jnp.concatenate(pieces, axis=1)
    return (left_acc, right_out, weight_acc, bias_acc)


def general(
    alignment,
    norm_mean,
    norm_inverse,
    norm_gain,
    norm_shift,
    input_weight,
    input_bias,
    output_weight,
    pair_cotangent,
    residue_mask,
    sequence_mask,
):
    sequence_count, residue_count = sequence_mask.shape
    residue_total = residue_mask.shape[0]
    column = lax.axis_index("col")
    residue_float = residue_mask.astype(jnp.float32)
    own_residues = lax.dynamic_slice_in_dim(residue_float, column * residue_count, residue_count, 0)
    own_mask = lax.dynamic_slice_in_dim(residue_mask, column * residue_count, residue_count, 0)
    live_int = sequence_mask * own_mask[None, :]
    live = live_int.astype(jnp.float32)
    hatted, normed = normalize(alignment, norm_mean, norm_inverse, norm_gain, norm_shift)
    projected = project(normed, input_weight, input_bias, live)
    left = projected[..., :P_SIZE]
    right = projected[..., P_SIZE:]
    gathered, mask_cols = (
        lax.all_gather(
            right.reshape(sequence_count, residue_count * P_SIZE), "col", axis=1, tiled=True
        ),
        lax.all_gather(live_int, "col", axis=1, tiled=True),
    )
    right_all = gathered.reshape(sequence_count, residue_total, P_SIZE)
    partial_counts = jnp.dot(live.T, mask_cols.astype(jnp.float32), precision=lax.Precision.HIGHEST)
    counts = lax.psum(partial_counts, "row")
    pair_live = own_residues[:, None] * residue_float[None, :]
    left_grad, right_part, weight_out, bias_out = contract(
        left, right_all, counts, pair_cotangent, pair_live, output_weight
    )
    bias_out = bias_out / lax.axis_size("row")
    summed = lax.psum_scatter(
        right_part.reshape(sequence_count, residue_total * P_SIZE),
        "col",
        scatter_dimension=1,
        tiled=True,
    )
    right_grad = summed.reshape(sequence_count, residue_count, P_SIZE)
    proj_grad = jnp.concatenate([left_grad, right_grad], axis=-1) * live[..., None]
    proj_low = proj_grad.astype(jnp.bfloat16).reshape(-1, 2 * P_SIZE)
    flat_normed = normed.reshape(-1, C)
    weight_part = jnp.einsum("nc,nk->ck", flat_normed, proj_low, preferred_element_type=jnp.float32)
    bias_part = jnp.sum(proj_grad, axis=(0, 1))
    normed_grad = jnp.einsum(
        "nk,ck->nc", proj_low, input_weight, preferred_element_type=jnp.float32
    ).reshape(hatted.shape)
    gain_part = jnp.sum(normed_grad * hatted, axis=(0, 1))
    shift_part = jnp.sum(normed_grad, axis=(0, 1))
    hat_grad = normed_grad * norm_gain
    centered = (
        hat_grad
        - jnp.mean(hat_grad, axis=-1, keepdims=True)
        - hatted * jnp.mean(hat_grad * hatted, axis=-1, keepdims=True)
    )
    activation_grad = (norm_inverse[..., None] * centered).astype(jnp.bfloat16)
    totals = lax.psum(
        (weight_part, bias_part, gain_part, shift_part, weight_out, bias_out), ("row", "col")
    )
    return (activation_grad, totals[0], totals[1], totals[4], totals[5], totals[2], totals[3])


LANES = 128
PROJ_ROWS = 256
COT_AT = 256
MESSAGE = 320
DEAD = 32768.0
SMALL_AT = 256
PARTIAL = 264
SENT = 272
PEERS = ((0, 6, 1, 5), (2, 4, 3, 7))
ORDER = (0, 6, 1, 7, 2, 5, 3, 4)
VMEM = pltpu.CompilerParams(vmem_limit_bytes=24 * 1024 * 1024)
F32 = jnp.float32
BF16 = jnp.bfloat16


def dot_nt(a, b):
    return lax.dot_general(a, b, (((1,), (1,)), ((), ())), preferred_element_type=F32)


def dot_nn(a, b):
    return lax.dot_general(a, b, (((1,), (0,)), ((), ())), preferred_element_type=F32)


def low_lanes(shape):
    return lax.broadcasted_iota(jnp.int32, shape, 1) < LANES // 2


def swap_halves(x):
    return pltpu.roll(x, LANES // 2, 1)


def strided(wide, start, size, stride):
    return jnp.concatenate([wide[h, pl.ds(start, size, stride=stride), :] for h in range(2)], axis=1)


def prepare(*rest):
    sources = rest[:11]
    gain, shift, weight, cotangent, out_weight, hat, stats, present = rest[11:19]
    messages = rest[19:-13]
    count = len(messages)
    alignment, mean, inverse, bias, residue, mask, wide, packed, cot, turned, square, arrived, late = rest[-13:]
    targets = (alignment, mean, inverse, bias, residue, mask, gain, shift, weight)
    first = pltpu.make_async_copy(sources[-2], cotangent, late.at[0])
    first.start()
    copies = [pltpu.make_async_copy(f, t, arrived.at[i]) for i, (f, t) in enumerate(zip(sources, targets))]
    for copy in copies:
        copy.start()
    last = pltpu.make_async_copy(sources[-1], out_weight, late.at[1])
    last.start()
    col, row = lax.axis_index("col"), lax.axis_index("row")
    seqs, own, channels = alignment.shape
    total = cotangent.shape[1]
    depth = Z // count
    first.wait()

    @pl.when(row == 0)
    def _():
        cot[...] = cotangent[...].astype(F32).reshape(own * total, Z)
        for k, message in enumerate(messages):
            peer = col ^ ORDER[k]
            block = square.at[k % 2 * own * own : (k % 2 + 1) * own * own, :]
            for i in range(own):
                block[i * own : (i + 1) * own, :] = cot[
                    pl.ds(pl.multiple_of(i * total + own * peer, own), own), :
                ]
            message[COT_AT:MESSAGE, :] = jnp.concatenate(
                [block[pl.ds(j, own, stride=own), :] for j in range(own)], axis=0
            ).astype(BF16)

    @pl.when(row != 0)
    def _():
        for i in range(own // 2):
            pair = jnp.concatenate([cotangent[i], cotangent[i + own // 2]], axis=0).astype(F32)
            turned[i] = pair.T.astype(BF16)
        for k, message in enumerate(messages):
            at = pl.multiple_of((col ^ ORDER[k]) * depth, depth)
            for i in range(own // 2):
                message[COT_AT + i * depth : COT_AT + (i + 1) * depth, :] = turned[i, pl.ds(at, depth), :]

    for copy in copies:
        copy.wait()
    square[0:own, :seqs] = mean[...]
    square[own : 2 * own, :seqs] = inverse[...]
    square[2 * own : 3 * own, : 2 * P_SIZE] = jnp.broadcast_to(bias[...], (own, 2 * P_SIZE))
    square[3 * own : 4 * own, :total] = jnp.broadcast_to(residue[...].astype(F32), (own, total))
    stats[...] = square[...].T
    present[...] = jnp.broadcast_to(stats[:total, 3 * own : 3 * own + 1], (total, LANES))
    live = mask[...].astype(F32) * present[pl.ds(pl.multiple_of(col * own, own), own), :seqs]
    values = alignment[...].astype(F32)
    for h in range(2):
        wide[h] = values[:, :, h * LANES : (h + 1) * LANES].reshape(seqs * own, LANES)
    for r in range(own):
        hatted = (strided(wide, r, seqs, own) - stats[:seqs, r : r + 1]) * stats[
            :seqs, own + r : own + r + 1
        ]
        hat[r] = hatted
        normed = (hatted * gain[...] + shift[...]).astype(BF16)
        projected = dot_nt(weight[...], normed) + stats[: 2 * P_SIZE, 2 * own : 2 * own + 1]
        projected = jnp.where(live[r : r + 1] > 0.0, projected, DEAD)
        packed[pl.ds(r, P_SIZE, stride=own), :] = jnp.concatenate(
            [projected[:P_SIZE], projected[P_SIZE:]], axis=1
        )
    shared = packed[...].astype(BF16)
    for message in messages:
        message[0:PROJ_ROWS, :] = shared
    last.wait()


def collect(*rest):
    messages, out = rest[:-2], rest[-2]
    live = rest[-1]
    col = lax.axis_index("col")
    count = len(messages)
    own = live.shape[0] // count
    for k, message in enumerate(messages):
        peer = col ^ ORDER[k]
        out[peer] = message[COT_AT:MESSAGE, :]
        here = message[0 : 2 * own, :].astype(F32)[:own]
        live[pl.ds(pl.multiple_of(peer * own, own), own), :] = jnp.where(here < 0.5 * DEAD, 1.0, 0.0)
    out[count] = live[...].astype(BF16)


def interleave(product, target, group, at):
    half = LANES // 2
    low = low_lanes((P_SIZE, LANES))
    for a in range(0, product.shape[0] // P_SIZE, 2):
        for b in range(0, group, 2):
            first = product[a * P_SIZE : (a + 1) * P_SIZE, b * half : (b + 2) * half]
            second = product[(a + 1) * P_SIZE : (a + 2) * P_SIZE, b * half : (b + 2) * half]
            lanes = slice((at + a) * half, (at + a + 2) * half)
            target[b * P_SIZE : (b + 1) * P_SIZE, lanes] = jnp.where(
                low, first, swap_halves(second)
            ).astype(BF16)
            target[(b + 1) * P_SIZE : (b + 2) * P_SIZE, lanes] = jnp.where(
                low, swap_halves(first), second
            ).astype(BF16)


BLOCK = 8
STEPS = 3


def arrange(out_weight, *rest):
    messages = rest[:-4]
    every, gathered, by_second, wide = rest[-4:]
    col = lax.axis_index("col")
    own = PROJ_ROWS // P_SIZE
    total = own * len(messages)
    wide[...] = out_weight[...].astype(F32)
    for k, message in enumerate(messages):
        at = pl.multiple_of((col ^ ORDER[k]) * own, own)
        block = message[0:PROJ_ROWS, :].astype(F32)
        block = jnp.where(block < 0.5 * DEAD, block, 0.0)
        for q in range(P_SIZE):
            every[pl.ds(q * total + at, own), :] = block[q * own : (q + 1) * own]
    for q in range(P_SIZE):
        by_second[q * P_SIZE : (q + 1) * P_SIZE, :] = wide[pl.ds(q, P_SIZE, stride=P_SIZE), :].astype(BF16)
    gathered[...] = every[...].astype(BF16)


def quad_members(quad):
    base = quad // 2 * 8 + quad % 2 * 2
    return ((base, base + 4), (base + 1, base + 5))


def take_turns(*tracks):
    results = [None] * len(tracks)
    going = set(range(len(tracks)))
    while going:
        for t, (track, steps) in enumerate(tracks):
            for _ in range(steps):
                if t in going:
                    try:
                        next(track)
                    except StopIteration as end:
                        results[t] = end.value
                        going.discard(t)
    return results


def sums_part(
    pieces, mate, cotangent, by_second, present, out_weight, every, gathered, hat, gain, shift, weight, normed_grads, keep, turned, grad_own, grad_turned, grad_slice, outer, scales, corner, mixed, lefts, square
):
    col, row = lax.axis_index("col"), lax.axis_index("row")
    count = pieces.shape[0] - 1
    own, seqs, channels = hat.shape
    total = grad_turned.shape[0] // own
    depth = Z // count
    half = LANES // 2
    pairs = own // 2
    mine = row == 0
    here = present[...].astype(BF16)
    counts = sum(
        dot_nt(m, jnp.concatenate([m, m], axis=0)) for m in (pieces[count], mate[count])
    )
    scales[...] = (
        dot_nt(here, jnp.concatenate([here, here], axis=0))
        * (1.0 / LANES)
        / jnp.maximum(counts * 0.5, 1.0)
    )
    own_at = pl.ds(pl.multiple_of(col * own, own), own)
    scale_own = dot_nt(here, present[own_at, :].astype(BF16)) * (1.0 / LANES)
    counts_own = jnp.zeros((total, own), F32)
    for m in (pieces, mate):
        square[0:total, :] = m[count].astype(F32)
        counts_own = counts_own + dot_nt(m[count], square[own_at, :].astype(BF16))
    scale_own = scale_own / jnp.maximum(counts_own * 0.5, 1.0)
    square[0:total, :] = pieces[count].astype(F32)
    live = square[own_at, :]
    low = low_lanes((own, LANES))
    bias_acc = jnp.zeros((depth, LANES), F32)
    for c in range(count):
        one, two = pieces[c].astype(F32), mate[c].astype(F32)
        block = jnp.where(mine, one, two)
        for j in range(own):
            turned[j * total + c * own : j * total + (c + 1) * own, :] = block[j * own : (j + 1) * own]
        block = jnp.where(mine, two, one)
        tile = scales[c * own : (c + 1) * own, :]
        tile = jnp.where(low, tile, jnp.concatenate([tile[pairs:], tile[:pairs]], axis=0))
        for i in range(pairs):
            piece = block[i * depth : (i + 1) * depth] * tile[i : i + 1, :]
            bias_acc = bias_acc + piece
            grad_slice[
                (c * 2 + i // 2) * depth : (c * 2 + i // 2 + 1) * depth,
                i % 2 * LANES : (i % 2 + 1) * LANES,
            ] = piece.astype(BF16)
    for i in range(own):
        rows = slice(i * total, (i + 1) * total)
        grad_own[rows, :] = (cotangent[i].astype(F32) * scale_own[:, i : i + 1]).astype(BF16)
        grad_turned[rows, :] = (turned[rows, :] * scale_own[:, i : i + 1]).astype(BF16)

    def grads():
        for a in range(0, P_SIZE, BLOCK):
            rows = slice(a * P_SIZE, (a + BLOCK) * P_SIZE)
            interleave(dot_nt(by_second[rows, :], grad_own[...]), outer.at[0], own, a)
            yield
        left_grad = swap_halves(dot_nn(outer[0], gathered[...]))
        yield
        for a in range(0, P_SIZE, BLOCK):
            rows = slice(a * P_SIZE, (a + BLOCK) * P_SIZE)
            interleave(dot_nt(out_weight[rows, :], grad_turned[...]), outer.at[1], own, a)
            yield
        right_grad = dot_nn(outer[1], gathered[...])
        yield
        input_acc = jnp.zeros((2 * P_SIZE, channels), F32)
        proj_acc = jnp.zeros((2 * P_SIZE, seqs), F32)
        gain_acc = jnp.zeros((1, channels), F32)
        shift_acc = jnp.zeros((1, channels), F32)
        for r in range(own):
            hatted = hat[r]
            normed = (hatted * gain[...] + shift[...]).astype(BF16)
            spot = slice(r * P_SIZE, (r + 1) * P_SIZE)
            proj_grad = jnp.concatenate([left_grad[spot, :seqs], right_grad[spot, :seqs]], axis=0)
            proj_grad = proj_grad * live[r : r + 1, :seqs]
            proj_acc = proj_acc + proj_grad
            input_acc = input_acc + dot_nn(proj_grad.astype(BF16), normed)
            normed_grad = dot_nn(proj_grad.T.astype(BF16), weight[...])
            gain_acc = gain_acc + jnp.sum(normed_grad * hatted, axis=0, keepdims=True)
            shift_acc = shift_acc + jnp.sum(normed_grad, axis=0, keepdims=True)
            normed_grads[r] = normed_grad
            yield
        return (input_acc, proj_acc, gain_acc, shift_acc)

    quads = count * own // 4

    def slices():
        low = low_lanes((total, LANES))
        corner[...] = jnp.zeros_like(corner)
        for q in range(P_SIZE):
            block = every[q * total : (q + 1) * total, :]
            here = jnp.where(low, 0.0, block)
            moved = swap_halves(here).astype(BF16)
            here = here.astype(BF16)
            slot = q % corner.shape[0]
            for at in range(4):
                lanes = slice(at // 2 * LANES, (at // 2 + 1) * LANES)
                corner[slot, at * total : (at + 1) * total, lanes] = here if at % 2 else moved
            product = dot_nn(grad_slice[...], corner[slot]).astype(BF16)
            for quad in range(quads):
                mixed[q * depth : (q + 1) * depth, quad * 4 * total : (quad + 1) * 4 * total] = product[
                    quad * depth : (quad + 1) * depth
                ]
            yield
        low = low_lanes((P_SIZE, LANES))
        rhs = []
        for quad in range(quads):
            for pair in quad_members(quad):
                one, two = (every[pl.ds(i, P_SIZE, stride=total), :] for i in pair)
                rhs.append(jnp.where(low, one, swap_halves(two)).astype(BF16))
        lefts[...] = jnp.concatenate(rhs, axis=1)
        yield
        weight_acc = []
        chunk = P_SIZE * depth // 2
        for b in range(2):
            weight_acc.append(dot_nt(mixed[b * chunk : (b + 1) * chunk, :], lefts[...]))
            yield
        weight_acc = jnp.concatenate(weight_acc, axis=0)
        return weight_acc

    (input_acc, proj_acc, gain_acc, shift_acc), weight_acc = take_turns((grads(), 1), (slices(), STEPS))
    group = P_SIZE * depth // 4
    weight_acc = jnp.concatenate([weight_acc[b * group : (b + 1) * group] for b in range(4)], axis=1)

    square[...] = jnp.zeros((LANES, LANES), F32)
    square[0 : 2 * P_SIZE, :seqs] = proj_acc
    square[half : half + depth, :] = bias_acc * 0.5
    sums = jnp.sum(square[...].T, axis=0, keepdims=True)
    keep[0:LANES, :] = weight_acc
    for h in range(2):
        lanes = slice(h * LANES, (h + 1) * LANES)
        keep[LANES + h * half : LANES + (h + 1) * half, :] = input_acc[:, lanes]
        keep[SMALL_AT + h : SMALL_AT + h + 1, :] = gain_acc[:, lanes]
        keep[SMALL_AT + 2 + h : SMALL_AT + 3 + h, :] = shift_acc[:, lanes]
    keep[SMALL_AT + 4 : PARTIAL, :] = jnp.concatenate([sums, jnp.zeros((3, LANES), F32)], axis=0)


def activations(normed_grads, hat, stats, gain, activation, wide):
    own, seqs, channels = hat.shape
    for r in range(own):
        hatted = hat[r]
        hat_grad = normed_grads[r] * gain[...]
        first = jnp.sum(hat_grad, axis=1, keepdims=True) * (1.0 / channels)
        second = jnp.sum(hat_grad * hatted, axis=1, keepdims=True) * (1.0 / channels)
        result = stats[:seqs, own + r : own + r + 1] * (hat_grad - first - hatted * second)
        for h in range(2):
            wide[h, pl.ds(r, seqs, stride=own), :] = result[:, h * LANES : (h + 1) * LANES]
    activation[...] = jnp.concatenate(
        [wide[h].reshape(seqs, own, LANES) for h in range(2)], axis=2
    ).astype(BF16)


def pack(kept, given, partial):
    both = kept[...] + given[...]
    high = both.astype(BF16)
    small = both[SMALL_AT:] - high[SMALL_AT:].astype(F32)
    partial[...] = jnp.concatenate([high, small.astype(BF16)], axis=0)


def stack(*rest):
    for k, part in enumerate(rest[:-1]):
        rest[-1][k] = part[...]


def finish(own, received, mate, input_out, bias_out, weight_out, out_bias_out, gain_out, shift_out, ordered):
    col, row = lax.axis_index("col"), lax.axis_index("row")
    count = ordered.shape[0]
    depth = Z // count
    half = LANES // 2
    lane = lax.broadcasted_iota(jnp.int32, (1, LANES), 1)
    ordered[col] = own[...]
    for k, (one, two) in enumerate(zip(*PEERS)):
        ordered[col ^ jnp.where(row == 0, one, two)] = received[k]
        ordered[col ^ jnp.where(row == 0, two, one)] = mate[k]
    ordered[col] = own[...]
    for a in range(8):
        turned = jnp.concatenate(
            [ordered[c, a * depth : (a + 1) * depth] for c in range(count)], axis=0
        ).astype(F32).T
        for b in range(4):
            weight_out[pl.ds(8 * b + a, P_SIZE, stride=P_SIZE), :] = turned[b * P_SIZE : (b + 1) * P_SIZE]
    input_acc = jnp.zeros((LANES, LANES), F32)
    small_acc = jnp.zeros((8, LANES), F32)
    out_bias = jnp.zeros((1, LANES), F32)
    for c in range(count):
        input_acc = input_acc + ordered[c, LANES:SMALL_AT].astype(F32)
        both = ordered[c, SMALL_AT:].astype(F32)
        small = both[:8] + both[8:]
        small_acc = small_acc + small
        bias = pltpu.roll(small[4:5], (c * depth + half) % LANES, 1)
        out_bias = jnp.where((lane >= c * depth) & (lane < (c + 1) * depth), bias, out_bias)
    for h in range(2):
        lanes = slice(h * LANES, (h + 1) * LANES)
        input_out[:, lanes] = input_acc[h * half : (h + 1) * half]
        gain_out[:, lanes] = small_acc[h : h + 1]
        shift_out[:, lanes] = small_acc[2 + h : 3 + h]
    bias_out[...] = small_acc[4:5, :half]
    out_bias_out[...] = out_bias


def shape(dims, dtype):
    return jax.ShapeDtypeStruct(dims, dtype)


VMEM_SPEC = pl.BlockSpec(memory_space=pltpu.VMEM)
HBM_SPEC = pl.BlockSpec(memory_space=pltpu.HBM)


def call(kernel, outputs, specs, arguments, scratch=(), aliases=None):
    return pl.pallas_call(
        kernel,
        out_shape=outputs,
        in_specs=specs,
        out_specs=[VMEM_SPEC] * len(outputs),
        scratch_shapes=list(scratch),
        input_output_aliases=aliases or {},
        compiler_params=VMEM,
        name=kernel.__name__,
    )(*arguments)


def tiled(
    alignment,
    norm_mean,
    norm_inverse,
    norm_gain,
    norm_shift,
    input_weight,
    input_bias,
    output_weight,
    pair_cotangent,
    residue_mask,
    sequence_mask,
):
    count = lax.axis_size("col")
    seqs, own, channels = alignment.shape
    total = pair_cotangent.shape[1]
    depth = Z // count
    turn = [(0, 1), (1, 0)]
    fetched = [alignment, norm_mean.T, norm_inverse.T, input_bias[None, :], residue_mask[None, :], sequence_mask.T]
    passed = [norm_gain[None, :], norm_shift[None, :], input_weight.T, pair_cotangent, output_weight]
    operands = [pltpu.with_memory_space_constraint(a, pltpu.HBM) for a in fetched + passed]
    gain, shift, weight, cotangent, out_weight, hat, stats, present, *messages = call(
        prepare,
        [shape(a.shape, a.dtype) for a in passed]
        + [shape((own, seqs, channels), F32), shape((LANES, LANES), F32), shape((total, LANES), F32)]
        + [shape((MESSAGE, LANES), BF16)] * count,
        [HBM_SPEC] * len(operands),
        operands,
        [pltpu.VMEM(a.shape, a.dtype) for a in fetched]
        + [
            pltpu.VMEM((2, seqs * own, LANES), F32),
            pltpu.VMEM((PROJ_ROWS, LANES), F32),
            pltpu.VMEM((own * total, Z), F32),
            pltpu.VMEM((own // 2, Z, LANES), BF16),
            pltpu.VMEM((LANES, LANES), F32),
            pltpu.SemaphoreType.DMA((len(operands) - 2,)),
            pltpu.SemaphoreType.DMA((2,)),
        ],
    )
    messages = [messages[0]] + [
        lax.ppermute(messages[k], "col", [(c, c ^ ORDER[k]) for c in range(count)]) for k in range(1, count)
    ]
    (pieces,) = call(
        collect,
        [shape((count + 1, total, LANES), BF16)],
        [VMEM_SPEC] * count,
        messages,
        [pltpu.VMEM((total, LANES), F32)],
    )
    mate_pieces = lax.ppermute(pieces, "row", turn)
    every, gathered, by_second = call(
        arrange,
        [
            shape((P_SIZE * total, LANES), F32),
            shape((P_SIZE * total, LANES), BF16),
            shape((P_SIZE * P_SIZE, LANES), BF16),
        ],
        [VMEM_SPEC] * (1 + count),
        [out_weight, *messages],
        [pltpu.VMEM((P_SIZE * P_SIZE, LANES), F32)],
    )
    normed_grads, keep = call(
        sums_part,
        [shape((own, seqs, channels), F32), shape((PARTIAL, LANES), F32)],
        [VMEM_SPEC] * 12,
        [pieces, mate_pieces, cotangent, by_second, present, out_weight, every, gathered, hat, gain, shift, weight],
        [
            pltpu.VMEM((own * total, Z), F32),
            pltpu.VMEM((own * total, Z), BF16),
            pltpu.VMEM((own * total, Z), BF16),
            pltpu.VMEM((count * own // 4 * depth, 2 * LANES), BF16),
            pltpu.VMEM((2, own * P_SIZE, P_SIZE * total), BF16),
            pltpu.VMEM((total, LANES), F32),
            pltpu.VMEM((4, 4 * total, 2 * LANES), BF16),
            pltpu.VMEM((P_SIZE * depth, count * own * seqs), BF16),
            pltpu.VMEM((P_SIZE, count * own * seqs), BF16),
            pltpu.VMEM((LANES, LANES), F32),
        ],
    )
    given = lax.ppermute(keep, "row", turn)
    (activation,) = call(
        activations,
        [shape(alignment.shape, BF16)],
        [VMEM_SPEC] * 4,
        [normed_grads, hat, stats, gain],
        [pltpu.VMEM((2, seqs * own, LANES), F32)],
    )
    (partial,) = call(
        pack, [shape((SENT, LANES), BF16)], [VMEM_SPEC] * 2, [keep, given]
    )
    parts = []
    for pair in zip(*PEERS):
        turns = [
            (row * count + c, row * count + (c ^ pair[row])) for row in range(2) if pair[row] for c in range(count)
        ]
        parts.append(lax.ppermute(partial, ("row", "col"), turns))
    (received,) = call(
        stack, [shape((len(parts), SENT, LANES), BF16)], [VMEM_SPEC] * len(parts), parts
    )
    theirs = lax.ppermute(received, "row", turn)
    input_grad, bias_grad, weight_grad, out_bias_grad, gain_grad, shift_grad = call(
        finish,
        [
            shape((2 * P_SIZE, channels), F32),
            shape((1, 2 * P_SIZE), F32),
            shape((P_SIZE * P_SIZE, Z), F32),
            shape((1, Z), F32),
            shape((1, channels), F32),
            shape((1, channels), F32),
        ],
        [VMEM_SPEC] * 3,
        [partial, received, theirs],
        [pltpu.VMEM((count, SENT, LANES), BF16)],
    )
    return (activation, input_grad.T, bias_grad[0], weight_grad, out_bias_grad[0], gain_grad[0], shift_grad[0])


def local(*args):
    alignment, cotangent = args[0], args[8]
    seqs, own, channels = alignment.shape
    total = cotangent.shape[1]
    count = lax.axis_size("col")
    fits = (
        2 * seqs == LANES
        and 2 * total == LANES
        and own == 8
        and channels == 2 * LANES
        and count == 8
        and lax.axis_size("row") == 2
    )
    return tiled(*args) if fits else general(*args)


def solution(mesh):
    in_specs = (
        P(("group", "row"), "col", None),
        P(("group", "row"), "col"),
        P(("group", "row"), "col"),
        P(),
        P(),
        P(),
        P(),
        P(),
        P("col", "group", None),
        P("group"),
        P(("group", "row"), "col"),
    )
    out_specs = (
        P(("group", "row"), "col", None),
        P("group", None),
        P("group"),
        P("group", None),
        P("group"),
        P("group"),
        P("group"),
    )
    return jax.shard_map(local, mesh=mesh, in_specs=in_specs, out_specs=out_specs, check_vma=False)
```

```python
import math

import jax
import jax.numpy as jnp
from jax import lax
from jax.experimental import pallas as pl
from jax.experimental.pallas import tpu as pltpu
from jax.sharding import PartitionSpec as P

C = 256
P_SIZE = 32
Z = 128


def normalize(alignment, norm_mean, norm_inverse, norm_gain, norm_shift):
    hatted = (alignment.astype(jnp.float32) - norm_mean[..., None]) * norm_inverse[..., None]
    normed = (hatted * norm_gain + norm_shift).astype(jnp.bfloat16)
    return (hatted, normed)


def project(normed, input_weight, input_bias, live):
    flat = normed.reshape(-1, normed.shape[-1])
    projected = jnp.dot(flat, input_weight, preferred_element_type=jnp.float32) + input_bias
    projected = projected.reshape(normed.shape[:-1] + (input_weight.shape[1],)) * live[..., None]
    return projected.astype(jnp.bfloat16)


def contract(left, right, counts, cotangent, pair_live, output_weight):
    sequence_count, row_count, _ = left.shape
    column_total = right.shape[1]
    width = math.gcd(column_total, 128)
    left_acc = jnp.zeros(left.shape, jnp.float32)
    weight_acc = jnp.zeros((P_SIZE * P_SIZE, Z), jnp.float32)
    bias_acc = jnp.zeros((Z,), jnp.float32)
    pieces = []
    for offset in range(0, column_total, width):
        right_cols = right[:, offset : offset + width]
        scale = pair_live[:, offset : offset + width] / jnp.maximum(
            counts[:, offset : offset + width], 1.0
        )
        pair_grad = cotangent[:, offset : offset + width].astype(jnp.float32) * scale[..., None]
        pair_low = pair_grad.astype(jnp.bfloat16).reshape(-1, Z)
        outer_grad = jnp.einsum(
            "ne,ke->nk", pair_low, output_weight, preferred_element_type=jnp.float32
        )
        outer_grad = outer_grad.astype(jnp.bfloat16).reshape(row_count, width, P_SIZE, P_SIZE)
        left_acc = left_acc + jnp.einsum(
            "ijpq,sjq->sip", outer_grad, right_cols, preferred_element_type=jnp.float32
        )
        pieces.append(
            jnp.einsum("ijpq,sip->sjq", outer_grad, left, preferred_element_type=jnp.float32)
        )
        outer = jnp.einsum(
            "sip,sjq->ijpq", left, right_cols, preferred_element_type=jnp.float32
        ).reshape(-1, P_SIZE * P_SIZE)
        outer_high = outer.astype(jnp.bfloat16)
        outer_rest = (outer - outer_high.astype(jnp.float32)).astype(jnp.bfloat16)
        weight_acc = weight_acc + jnp.einsum(
            "nk,ne->ke", outer_high, pair_low, preferred_element_type=jnp.float32
        )
        weight_acc = weight_acc + jnp.einsum(
            "nk,ne->ke", outer_rest, pair_low, preferred_element_type=jnp.float32
        )
        bias_acc = bias_acc + jnp.sum(pair_grad, axis=(0, 1))
    right_out = jnp.concatenate(pieces, axis=1)
    return (left_acc, right_out, weight_acc, bias_acc)


def general(
    alignment,
    norm_mean,
    norm_inverse,
    norm_gain,
    norm_shift,
    input_weight,
    input_bias,
    output_weight,
    pair_cotangent,
    residue_mask,
    sequence_mask,
):
    sequence_count, residue_count = sequence_mask.shape
    residue_total = residue_mask.shape[0]
    column = lax.axis_index("col")
    residue_float = residue_mask.astype(jnp.float32)
    own_residues = lax.dynamic_slice_in_dim(residue_float, column * residue_count, residue_count, 0)
    own_mask = lax.dynamic_slice_in_dim(residue_mask, column * residue_count, residue_count, 0)
    live_int = sequence_mask * own_mask[None, :]
    live = live_int.astype(jnp.float32)
    hatted, normed = normalize(alignment, norm_mean, norm_inverse, norm_gain, norm_shift)
    projected = project(normed, input_weight, input_bias, live)
    left = projected[..., :P_SIZE]
    right = projected[..., P_SIZE:]
    gathered, mask_cols = (
        lax.all_gather(
            right.reshape(sequence_count, residue_count * P_SIZE), "col", axis=1, tiled=True
        ),
        lax.all_gather(live_int, "col", axis=1, tiled=True),
    )
    right_all = gathered.reshape(sequence_count, residue_total, P_SIZE)
    partial_counts = jnp.dot(live.T, mask_cols.astype(jnp.float32), precision=lax.Precision.HIGHEST)
    counts = lax.psum(partial_counts, "row")
    pair_live = own_residues[:, None] * residue_float[None, :]
    left_grad, right_part, weight_out, bias_out = contract(
        left, right_all, counts, pair_cotangent, pair_live, output_weight
    )
    bias_out = bias_out / lax.axis_size("row")
    summed = lax.psum_scatter(
        right_part.reshape(sequence_count, residue_total * P_SIZE),
        "col",
        scatter_dimension=1,
        tiled=True,
    )
    right_grad = summed.reshape(sequence_count, residue_count, P_SIZE)
    proj_grad = jnp.concatenate([left_grad, right_grad], axis=-1) * live[..., None]
    proj_low = proj_grad.astype(jnp.bfloat16).reshape(-1, 2 * P_SIZE)
    flat_normed = normed.reshape(-1, C)
    weight_part = jnp.einsum("nc,nk->ck", flat_normed, proj_low, preferred_element_type=jnp.float32)
    bias_part = jnp.sum(proj_grad, axis=(0, 1))
    normed_grad = jnp.einsum(
        "nk,ck->nc", proj_low, input_weight, preferred_element_type=jnp.float32
    ).reshape(hatted.shape)
    gain_part = jnp.sum(normed_grad * hatted, axis=(0, 1))
    shift_part = jnp.sum(normed_grad, axis=(0, 1))
    hat_grad = normed_grad * norm_gain
    centered = (
        hat_grad
        - jnp.mean(hat_grad, axis=-1, keepdims=True)
        - hatted * jnp.mean(hat_grad * hatted, axis=-1, keepdims=True)
    )
    activation_grad = (norm_inverse[..., None] * centered).astype(jnp.bfloat16)
    totals = lax.psum(
        (weight_part, bias_part, gain_part, shift_part, weight_out, bias_out), ("row", "col")
    )
    return (activation_grad, totals[0], totals[1], totals[4], totals[5], totals[2], totals[3])


LANES = 128
PROJ_ROWS = 256
COT_AT = 256
MESSAGE = 320
DEAD = 32768.0
SMALL_AT = 256
PARTIAL = 264
SENT = 272
PEERS = ((0, 6, 1, 5), (2, 4, 3, 7))
ORDER = (0, 6, 1, 7, 2, 5, 3, 4)
VMEM = pltpu.CompilerParams(vmem_limit_bytes=24 * 1024 * 1024)
F32 = jnp.float32
BF16 = jnp.bfloat16


def dot_nt(a, b):
    return lax.dot_general(a, b, (((1,), (1,)), ((), ())), preferred_element_type=F32)


def dot_nn(a, b):
    return lax.dot_general(a, b, (((1,), (0,)), ((), ())), preferred_element_type=F32)


def low_lanes(shape):
    return lax.broadcasted_iota(jnp.int32, shape, 1) < LANES // 2


def swap_halves(x):
    return pltpu.roll(x, LANES // 2, 1)


def strided(wide, start, size, stride):
    return jnp.concatenate([wide[h, pl.ds(start, size, stride=stride), :] for h in range(2)], axis=1)


def prepare(*rest):
    sources = rest[:11]
    gain, shift, weight, cotangent, out_weight, hat, stats, present = rest[11:19]
    messages = rest[19:-13]
    count = len(messages)
    alignment, mean, inverse, bias, residue, mask, wide, packed, cot, turned, square, arrived, late = rest[-13:]
    targets = (alignment, mean, inverse, bias, residue, mask, gain, shift, weight)
    first = pltpu.make_async_copy(sources[-2], cotangent, late.at[0])
    first.start()
    copies = [pltpu.make_async_copy(f, t, arrived.at[i]) for i, (f, t) in enumerate(zip(sources, targets))]
    for copy in copies:
        copy.start()
    last = pltpu.make_async_copy(sources[-1], out_weight, late.at[1])
    last.start()
    col, row = lax.axis_index("col"), lax.axis_index("row")
    seqs, own, channels = alignment.shape
    total = cotangent.shape[1]
    depth = Z // count
    for copy in copies:
        copy.wait()
    square[0:own, :seqs] = mean[...]
    square[own : 2 * own, :seqs] = inverse[...]
    square[2 * own : 3 * own, : 2 * P_SIZE] = jnp.broadcast_to(bias[...], (own, 2 * P_SIZE))
    square[3 * own : 4 * own, :total] = jnp.broadcast_to(residue[...].astype(F32), (own, total))
    stats[...] = square[...].T
    present[...] = jnp.broadcast_to(stats[:total, 3 * own : 3 * own + 1], (total, LANES))
    live = mask[...].astype(F32) * present[pl.ds(pl.multiple_of(col * own, own), own), :seqs]
    values = alignment[...].astype(F32)
    for h in range(2):
        wide[h] = values[:, :, h * LANES : (h + 1) * LANES].reshape(seqs * own, LANES)
    for r in range(own):
        hatted = (strided(wide, r, seqs, own) - stats[:seqs, r : r + 1]) * stats[
            :seqs, own + r : own + r + 1
        ]
        hat[r] = hatted
        normed = (hatted * gain[...] + shift[...]).astype(BF16)
        projected = dot_nt(weight[...], normed) + stats[: 2 * P_SIZE, 2 * own : 2 * own + 1]
        projected = jnp.where(live[r : r + 1] > 0.0, projected, DEAD)
        packed[pl.ds(r, P_SIZE, stride=own), :] = jnp.concatenate(
            [projected[:P_SIZE], projected[P_SIZE:]], axis=1
        )
    shared = packed[...].astype(BF16)
    for message in messages:
        message[0:PROJ_ROWS, :] = shared
    first.wait()

    @pl.when(row == 0)
    def _():
        cot[...] = cotangent[...].astype(F32).reshape(own * total, Z)
        for k, message in enumerate(messages):
            peer = col ^ ORDER[k]
            block = square.at[k % 2 * own * own : (k % 2 + 1) * own * own, :]
            for i in range(own):
                block[i * own : (i + 1) * own, :] = cot[
                    pl.ds(pl.multiple_of(i * total + own * peer, own), own), :
                ]
            message[COT_AT:MESSAGE, :] = jnp.concatenate(
                [block[pl.ds(j, own, stride=own), :] for j in range(own)], axis=0
            ).astype(BF16)

    @pl.when(row != 0)
    def _():
        for i in range(own // 2):
            pair = jnp.concatenate([cotangent[i], cotangent[i + own // 2]], axis=0).astype(F32)
            turned[i] = pair.T.astype(BF16)
        for k, message in enumerate(messages):
            at = pl.multiple_of((col ^ ORDER[k]) * depth, depth)
            for i in range(own // 2):
                message[COT_AT + i * depth : COT_AT + (i + 1) * depth, :] = turned[i, pl.ds(at, depth), :]

    last.wait()


def collect(*rest):
    messages, out = rest[:-2], rest[-2]
    live = rest[-1]
    col = lax.axis_index("col")
    count = len(messages)
    own = live.shape[0] // count
    for k, message in enumerate(messages):
        peer = col ^ ORDER[k]
        out[peer] = message[COT_AT:MESSAGE, :]
        here = message[0 : 2 * own, :].astype(F32)[:own]
        live[pl.ds(pl.multiple_of(peer * own, own), own), :] = jnp.where(here < 0.5 * DEAD, 1.0, 0.0)
    out[count] = live[...].astype(BF16)


def interleave(product, target, group, at):
    half = LANES // 2
    low = low_lanes((P_SIZE, LANES))
    for a in range(0, product.shape[0] // P_SIZE, 2):
        for b in range(0, group, 2):
            first = product[a * P_SIZE : (a + 1) * P_SIZE, b * half : (b + 2) * half]
            second = product[(a + 1) * P_SIZE : (a + 2) * P_SIZE, b * half : (b + 2) * half]
            lanes = slice((at + a) * half, (at + a + 2) * half)
            target[b * P_SIZE : (b + 1) * P_SIZE, lanes] = jnp.where(
                low, first, swap_halves(second)
            ).astype(BF16)
            target[(b + 1) * P_SIZE : (b + 2) * P_SIZE, lanes] = jnp.where(
                low, swap_halves(first), second
            ).astype(BF16)


BLOCK = 8
STEPS = 3


def arrange(out_weight, *rest):
    messages = rest[:-4]
    every, gathered, by_second, wide = rest[-4:]
    col = lax.axis_index("col")
    own = PROJ_ROWS // P_SIZE
    total = own * len(messages)
    wide[...] = out_weight[...].astype(F32)
    for k, message in enumerate(messages):
        at = pl.multiple_of((col ^ ORDER[k]) * own, own)
        block = message[0:PROJ_ROWS, :].astype(F32)
        block = jnp.where(block < 0.5 * DEAD, block, 0.0)
        for q in range(P_SIZE):
            every[pl.ds(q * total + at, own), :] = block[q * own : (q + 1) * own]
    for q in range(P_SIZE):
        by_second[q * P_SIZE : (q + 1) * P_SIZE, :] = wide[pl.ds(q, P_SIZE, stride=P_SIZE), :].astype(BF16)
    gathered[...] = every[...].astype(BF16)


def quad_members(quad):
    base = quad // 2 * 8 + quad % 2 * 2
    return ((base, base + 4), (base + 1, base + 5))


def take_turns(*tracks):
    results = [None] * len(tracks)
    going = set(range(len(tracks)))
    while going:
        for t, (track, steps) in enumerate(tracks):
            for _ in range(steps):
                if t in going:
                    try:
                        next(track)
                    except StopIteration as end:
                        results[t] = end.value
                        going.discard(t)
    return results


def sums_part(
    pieces, mate, cotangent, by_second, present, out_weight, every, gathered, hat, gain, shift, weight, normed_grads, keep, turned, grad_own, grad_turned, grad_slice, outer, scales, corner, mixed, lefts, square
):
    col, row = lax.axis_index("col"), lax.axis_index("row")
    count = pieces.shape[0] - 1
    own, seqs, channels = hat.shape
    total = grad_turned.shape[0] // own
    depth = Z // count
    half = LANES // 2
    pairs = own // 2
    mine = row == 0
    here = present[...].astype(BF16)
    counts = sum(
        dot_nt(m, jnp.concatenate([m, m], axis=0)) for m in (pieces[count], mate[count])
    )
    scales[...] = (
        dot_nt(here, jnp.concatenate([here, here], axis=0))
        * (1.0 / LANES)
        / jnp.maximum(counts * 0.5, 1.0)
    )
    own_at = pl.ds(pl.multiple_of(col * own, own), own)
    scale_own = dot_nt(here, present[own_at, :].astype(BF16)) * (1.0 / LANES)
    counts_own = jnp.zeros((total, own), F32)
    for m in (pieces, mate):
        square[0:total, :] = m[count].astype(F32)
        counts_own = counts_own + dot_nt(m[count], square[own_at, :].astype(BF16))
    scale_own = scale_own / jnp.maximum(counts_own * 0.5, 1.0)
    square[0:total, :] = pieces[count].astype(F32)
    live = square[own_at, :]
    low = low_lanes((own, LANES))
    bias_acc = jnp.zeros((depth, LANES), F32)
    for c in range(count):
        one, two = pieces[c].astype(F32), mate[c].astype(F32)
        block = jnp.where(mine, one, two)
        for j in range(own):
            turned[j * total + c * own : j * total + (c + 1) * own, :] = block[j * own : (j + 1) * own]
        block = jnp.where(mine, two, one)
        tile = scales[c * own : (c + 1) * own, :]
        tile = jnp.where(low, tile, jnp.concatenate([tile[pairs:], tile[:pairs]], axis=0))
        for i in range(pairs):
            piece = block[i * depth : (i + 1) * depth] * tile[i : i + 1, :]
            bias_acc = bias_acc + piece
            grad_slice[
                (c * 2 + i // 2) * depth : (c * 2 + i // 2 + 1) * depth,
                i % 2 * LANES : (i % 2 + 1) * LANES,
            ] = piece.astype(BF16)
    for i in range(own):
        rows = slice(i * total, (i + 1) * total)
        grad_own[rows, :] = (cotangent[i].astype(F32) * scale_own[:, i : i + 1]).astype(BF16)
        grad_turned[rows, :] = (turned[rows, :] * scale_own[:, i : i + 1]).astype(BF16)

    def grads():
        for a in range(0, P_SIZE, BLOCK):
            rows = slice(a * P_SIZE, (a + BLOCK) * P_SIZE)
            interleave(dot_nt(by_second[rows, :], grad_own[...]), outer.at[0], own, a)
            yield
        left_grad = swap_halves(dot_nn(outer[0], gathered[...]))
        yield
        for a in range(0, P_SIZE, BLOCK):
            rows = slice(a * P_SIZE, (a + BLOCK) * P_SIZE)
            interleave(dot_nt(out_weight[rows, :], grad_turned[...]), outer.at[1], own, a)
            yield
        right_grad = dot_nn(outer[1], gathered[...])
        yield
        input_acc = jnp.zeros((2 * P_SIZE, channels), F32)
        proj_acc = jnp.zeros((2 * P_SIZE, seqs), F32)
        gain_acc = jnp.zeros((1, channels), F32)
        shift_acc = jnp.zeros((1, channels), F32)
        for r in range(own):
            hatted = hat[r]
            normed = (hatted * gain[...] + shift[...]).astype(BF16)
            spot = slice(r * P_SIZE, (r + 1) * P_SIZE)
            proj_grad = jnp.concatenate([left_grad[spot, :seqs], right_grad[spot, :seqs]], axis=0)
            proj_grad = proj_grad * live[r : r + 1, :seqs]
            proj_acc = proj_acc + proj_grad
            input_acc = input_acc + dot_nn(proj_grad.astype(BF16), normed)
            normed_grad = dot_nn(proj_grad.T.astype(BF16), weight[...])
            gain_acc = gain_acc + jnp.sum(normed_grad * hatted, axis=0, keepdims=True)
            shift_acc = shift_acc + jnp.sum(normed_grad, axis=0, keepdims=True)
            normed_grads[r] = normed_grad
            yield
        return (input_acc, proj_acc, gain_acc, shift_acc)

    quads = count * own // 4

    def slices():
        low = low_lanes((total, LANES))
        corner[...] = jnp.zeros_like(corner)
        for q in range(P_SIZE):
            block = every[q * total : (q + 1) * total, :]
            here = jnp.where(low, 0.0, block)
            moved = swap_halves(here).astype(BF16)
            here = here.astype(BF16)
            slot = q % corner.shape[0]
            for at in range(4):
                lanes = slice(at // 2 * LANES, (at // 2 + 1) * LANES)
                corner[slot, at * total : (at + 1) * total, lanes] = here if at % 2 else moved
            product = dot_nn(grad_slice[...], corner[slot]).astype(BF16)
            for quad in range(quads):
                mixed[q * depth : (q + 1) * depth, quad * 4 * total : (quad + 1) * 4 * total] = product[
                    quad * depth : (quad + 1) * depth
                ]
            yield
        low = low_lanes((P_SIZE, LANES))
        rhs = []
        for quad in range(quads):
            for pair in quad_members(quad):
                one, two = (every[pl.ds(i, P_SIZE, stride=total), :] for i in pair)
                rhs.append(jnp.where(low, one, swap_halves(two)).astype(BF16))
        lefts[...] = jnp.concatenate(rhs, axis=1)
        yield
        weight_acc = []
        chunk = P_SIZE * depth // 2
        for b in range(2):
            weight_acc.append(dot_nt(mixed[b * chunk : (b + 1) * chunk, :], lefts[...]))
            yield
        weight_acc = jnp.concatenate(weight_acc, axis=0)
        return weight_acc

    (input_acc, proj_acc, gain_acc, shift_acc), weight_acc = take_turns((grads(), 1), (slices(), STEPS))
    group = P_SIZE * depth // 4
    weight_acc = jnp.concatenate([weight_acc[b * group : (b + 1) * group] for b in range(4)], axis=1)

    square[...] = jnp.zeros((LANES, LANES), F32)
    square[0 : 2 * P_SIZE, :seqs] = proj_acc
    square[half : half + depth, :] = bias_acc * 0.5
    sums = jnp.sum(square[...].T, axis=0, keepdims=True)
    keep[0:LANES, :] = weight_acc
    for h in range(2):
        lanes = slice(h * LANES, (h + 1) * LANES)
        keep[LANES + h * half : LANES + (h + 1) * half, :] = input_acc[:, lanes]
        keep[SMALL_AT + h : SMALL_AT + h + 1, :] = gain_acc[:, lanes]
        keep[SMALL_AT + 2 + h : SMALL_AT + 3 + h, :] = shift_acc[:, lanes]
    keep[SMALL_AT + 4 : PARTIAL, :] = jnp.concatenate([sums, jnp.zeros((3, LANES), F32)], axis=0)


def activations(normed_grads, hat, stats, gain, activation, wide):
    own, seqs, channels = hat.shape
    for r in range(own):
        hatted = hat[r]
        hat_grad = normed_grads[r] * gain[...]
        first = jnp.sum(hat_grad, axis=1, keepdims=True) * (1.0 / channels)
        second = jnp.sum(hat_grad * hatted, axis=1, keepdims=True) * (1.0 / channels)
        result = stats[:seqs, own + r : own + r + 1] * (hat_grad - first - hatted * second)
        for h in range(2):
            wide[h, pl.ds(r, seqs, stride=own), :] = result[:, h * LANES : (h + 1) * LANES]
    activation[...] = jnp.concatenate(
        [wide[h].reshape(seqs, own, LANES) for h in range(2)], axis=2
    ).astype(BF16)


def pack(kept, given, partial):
    both = kept[...] + given[...]
    high = both.astype(BF16)
    small = both[SMALL_AT:] - high[SMALL_AT:].astype(F32)
    partial[...] = jnp.concatenate([high, small.astype(BF16)], axis=0)


def stack(*rest):
    for k, part in enumerate(rest[:-1]):
        rest[-1][k] = part[...]


def finish(own, received, mate, input_out, bias_out, weight_out, out_bias_out, gain_out, shift_out, ordered):
    col, row = lax.axis_index("col"), lax.axis_index("row")
    count = ordered.shape[0]
    depth = Z // count
    half = LANES // 2
    lane = lax.broadcasted_iota(jnp.int32, (1, LANES), 1)
    ordered[col] = own[...]
    for k, (one, two) in enumerate(zip(*PEERS)):
        ordered[col ^ jnp.where(row == 0, one, two)] = received[k]
        ordered[col ^ jnp.where(row == 0, two, one)] = mate[k]
    ordered[col] = own[...]
    for a in range(8):
        turned = jnp.concatenate(
            [ordered[c, a * depth : (a + 1) * depth] for c in range(count)], axis=0
        ).astype(F32).T
        for b in range(4):
            weight_out[pl.ds(8 * b + a, P_SIZE, stride=P_SIZE), :] = turned[b * P_SIZE : (b + 1) * P_SIZE]
    input_acc = jnp.zeros((LANES, LANES), F32)
    small_acc = jnp.zeros((8, LANES), F32)
    out_bias = jnp.zeros((1, LANES), F32)
    for c in range(count):
        input_acc = input_acc + ordered[c, LANES:SMALL_AT].astype(F32)
        both = ordered[c, SMALL_AT:].astype(F32)
        small = both[:8] + both[8:]
        small_acc = small_acc + small
        bias = pltpu.roll(small[4:5], (c * depth + half) % LANES, 1)
        out_bias = jnp.where((lane >= c * depth) & (lane < (c + 1) * depth), bias, out_bias)
    for h in range(2):
        lanes = slice(h * LANES, (h + 1) * LANES)
        input_out[:, lanes] = input_acc[h * half : (h + 1) * half]
        gain_out[:, lanes] = small_acc[h : h + 1]
        shift_out[:, lanes] = small_acc[2 + h : 3 + h]
    bias_out[...] = small_acc[4:5, :half]
    out_bias_out[...] = out_bias


def shape(dims, dtype):
    return jax.ShapeDtypeStruct(dims, dtype)


VMEM_SPEC = pl.BlockSpec(memory_space=pltpu.VMEM)
HBM_SPEC = pl.BlockSpec(memory_space=pltpu.HBM)


def call(kernel, outputs, specs, arguments, scratch=(), aliases=None):
    return pl.pallas_call(
        kernel,
        out_shape=outputs,
        in_specs=specs,
        out_specs=[VMEM_SPEC] * len(outputs),
        scratch_shapes=list(scratch),
        input_output_aliases=aliases or {},
        compiler_params=VMEM,
        name=kernel.__name__,
    )(*arguments)


def tiled(
    alignment,
    norm_mean,
    norm_inverse,
    norm_gain,
    norm_shift,
    input_weight,
    input_bias,
    output_weight,
    pair_cotangent,
    residue_mask,
    sequence_mask,
):
    count = lax.axis_size("col")
    seqs, own, channels = alignment.shape
    total = pair_cotangent.shape[1]
    depth = Z // count
    turn = [(0, 1), (1, 0)]
    fetched = [alignment, norm_mean.T, norm_inverse.T, input_bias[None, :], residue_mask[None, :], sequence_mask.T]
    passed = [norm_gain[None, :], norm_shift[None, :], input_weight.T, pair_cotangent, output_weight]
    operands = [pltpu.with_memory_space_constraint(a, pltpu.HBM) for a in fetched + passed]
    gain, shift, weight, cotangent, out_weight, hat, stats, present, *messages = call(
        prepare,
        [shape(a.shape, a.dtype) for a in passed]
        + [shape((own, seqs, channels), F32), shape((LANES, LANES), F32), shape((total, LANES), F32)]
        + [shape((MESSAGE, LANES), BF16)] * count,
        [HBM_SPEC] * len(operands),
        operands,
        [pltpu.VMEM(a.shape, a.dtype) for a in fetched]
        + [
            pltpu.VMEM((2, seqs * own, LANES), F32),
            pltpu.VMEM((PROJ_ROWS, LANES), F32),
            pltpu.VMEM((own * total, Z), F32),
            pltpu.VMEM((own // 2, Z, LANES), BF16),
            pltpu.VMEM((LANES, LANES), F32),
            pltpu.SemaphoreType.DMA((len(operands) - 2,)),
            pltpu.SemaphoreType.DMA((2,)),
        ],
    )
    messages = [messages[0]] + [
        lax.ppermute(messages[k], "col", [(c, c ^ ORDER[k]) for c in range(count)]) for k in range(1, count)
    ]
    (pieces,) = call(
        collect,
        [shape((count + 1, total, LANES), BF16)],
        [VMEM_SPEC] * count,
        messages,
        [pltpu.VMEM((total, LANES), F32)],
    )
    mate_pieces = lax.ppermute(pieces, "row", turn)
    every, gathered, by_second = call(
        arrange,
        [
            shape((P_SIZE * total, LANES), F32),
            shape((P_SIZE * total, LANES), BF16),
            shape((P_SIZE * P_SIZE, LANES), BF16),
        ],
        [VMEM_SPEC] * (1 + count),
        [out_weight, *messages],
        [pltpu.VMEM((P_SIZE * P_SIZE, LANES), F32)],
    )
    normed_grads, keep = call(
        sums_part,
        [shape((own, seqs, channels), F32), shape((PARTIAL, LANES), F32)],
        [VMEM_SPEC] * 12,
        [pieces, mate_pieces, cotangent, by_second, present, out_weight, every, gathered, hat, gain, shift, weight],
        [
            pltpu.VMEM((own * total, Z), F32),
            pltpu.VMEM((own * total, Z), BF16),
            pltpu.VMEM((own * total, Z), BF16),
            pltpu.VMEM((count * own // 4 * depth, 2 * LANES), BF16),
            pltpu.VMEM((2, own * P_SIZE, P_SIZE * total), BF16),
            pltpu.VMEM((total, LANES), F32),
            pltpu.VMEM((4, 4 * total, 2 * LANES), BF16),
            pltpu.VMEM((P_SIZE * depth, count * own * seqs), BF16),
            pltpu.VMEM((P_SIZE, count * own * seqs), BF16),
            pltpu.VMEM((LANES, LANES), F32),
        ],
    )
    given = lax.ppermute(keep, "row", turn)
    (activation,) = call(
        activations,
        [shape(alignment.shape, BF16)],
        [VMEM_SPEC] * 4,
        [normed_grads, hat, stats, gain],
        [pltpu.VMEM((2, seqs * own, LANES), F32)],
    )
    (partial,) = call(
        pack, [shape((SENT, LANES), BF16)], [VMEM_SPEC] * 2, [keep, given]
    )
    parts = []
    for pair in zip(*PEERS):
        turns = [
            (row * count + c, row * count + (c ^ pair[row])) for row in range(2) if pair[row] for c in range(count)
        ]
        parts.append(lax.ppermute(partial, ("row", "col"), turns))
    parts[-1], activation = lax.optimization_barrier((parts[-1], activation))
    (received,) = call(
        stack, [shape((len(parts), SENT, LANES), BF16)], [VMEM_SPEC] * len(parts), parts
    )
    theirs = lax.ppermute(received, "row", turn)
    input_grad, bias_grad, weight_grad, out_bias_grad, gain_grad, shift_grad = call(
        finish,
        [
            shape((2 * P_SIZE, channels), F32),
            shape((1, 2 * P_SIZE), F32),
            shape((P_SIZE * P_SIZE, Z), F32),
            shape((1, Z), F32),
            shape((1, channels), F32),
            shape((1, channels), F32),
        ],
        [VMEM_SPEC] * 3,
        [partial, received, theirs],
        [pltpu.VMEM((count, SENT, LANES), BF16)],
    )
    return (activation, input_grad.T, bias_grad[0], weight_grad, out_bias_grad[0], gain_grad[0], shift_grad[0])


def local(*args):
    alignment, cotangent = args[0], args[8]
    seqs, own, channels = alignment.shape
    total = cotangent.shape[1]
    count = lax.axis_size("col")
    fits = (
        2 * seqs == LANES
        and 2 * total == LANES
        and own == 8
        and channels == 2 * LANES
        and count == 8
        and lax.axis_size("row") == 2
    )
    return tiled(*args) if fits else general(*args)


def solution(mesh):
    in_specs = (
        P(("group", "row"), "col", None),
        P(("group", "row"), "col"),
        P(("group", "row"), "col"),
        P(),
        P(),
        P(),
        P(),
        P(),
        P("col", "group", None),
        P("group"),
        P(("group", "row"), "col"),
    )
    out_specs = (
        P(("group", "row"), "col", None),
        P("group", None),
        P("group"),
        P("group", None),
        P("group"),
        P("group"),
        P("group"),
    )
    return jax.shard_map(local, mesh=mesh, in_specs=in_specs, out_specs=out_specs, check_vma=False)
```
